32 devices in a mesh: groups: 2 (over y), cache: 4 (over z), blk: 4 (over x, core).
Axes of the slice: x: 2, y: 2, z: 4, core: 2. Of those that a mesh axis runs over, the one named last changes fastest.
Arguments:
- queries: bfloat16 [8, 512, 2048], P(('groups', 'cache'), 'blk'), parts along dimension 0, may hold values from -6 to 6
- kv_new: bfloat16 [8, 512, 1024], P(('groups', 'cache'), 'blk'), parts along dimension 0, may hold values from -6 to 6
- page_pool: bfloat16 [8, 128, 8, 1024], P(('groups', 'cache')), parts along dimension 0, may hold values from -6 to 6
- page_owner: int32 [8, 4, 32, 1], P(('groups', 'cache'), 'blk'), parts along dimension 0, may hold values from 0 to 3; in each aligned block of 32 rows (0 to 31, 32 to 63, ..., all dimensions but the last counted through in order) at most 16 rows name the same one
- page_slot: int32 [8, 4, 32], P(('groups', 'cache'), 'blk'), parts along dimension 0, may hold values from 0 to 127
- prefix_len: int32 [8], P(('groups', 'cache')), parts along dimension 0, may hold values from 1 to 1024, 2048 in all
- suffix_len: int32 [8], P(('groups', 'cache')), parts along dimension 0, may hold values from 1 to 512, 1536 in all
- ssm_in: bfloat16 [8, 512, 2048], P(('groups', 'cache'), 'blk'), parts along dimension 0, may hold values from -6 to 6
- b_in: bfloat16 [8, 512, 128], P(('groups', 'cache'), 'blk'), parts along dimension 0, may hold values from -4 to 4
- c_in: bfloat16 [8, 512, 128], P(('groups', 'cache'), 'blk'), parts along dimension 0, may hold values from -4 to 4
- step_size: float32 [8, 512, 32], P(('groups', 'cache'), 'blk'), parts along dimension 0, may hold values from 0.01 to 0.1
- decay_rate: float32 [32], replicated, may hold values from 0.001953125 to 4
- skip_gain: float32 [32], replicated, may hold values from 0.5 to 1.5
- prior_state: float32 [8, 32, 64, 128], P(('groups', 'cache')), parts along dimension 0, may hold values from -4 to 4
Outputs:
- attn_out: bfloat16 [8, 512, 2048], P(('groups', 'cache'), 'blk'), parts along dimension 0
- ssm_out: bfloat16 [8, 512, 2048], P(('groups', 'cache'), 'blk'), parts along dimension 0
The draws below stay inside these ranges and needn't reach their ends.
There are 2 independent parts, one for each index of `groups`. The reference program is written for one: setup_inputs(seed, part) draws one part's arguments, and reference() takes and returns one part's arrays. A program takes and returns all parts, laid end to end along the dimension named above; an argument that names none is the same for every part. Nothing has to cross between parts.
Inputs may be any that keep to these rules, and one draw needn't show every extreme that they name: `page_owner`: among the 32 pages of one request at one index of blk, no owner is named more than 16 times, a bound that some block reaches. `prefix_len`: the largest is 1024. `suffix_len`: the largest is 512.
All inputs are finite; a program needn't handle non-finite values. No bound on the sum of `prefix_len` or of `suffix_len` on one device may be relied on, other than what follows from the above.
Results may differ from the reference program's by a relative error of at most 0.008.
Values may be sent and summed in bfloat16 or wider, within the bound.
A program may use at most 128 MiB of HBM per device.

```python
import math
import jax
import jax.numpy as jnp
import numpy as np
from jax import lax

QH = 16
KVH = 4
HD = 128
SH = 32
HP = 64
NS = 128
PAGE = 8
SUF_DEV = 128
LIST = 32
REQ = 4
SUF = 512
PREF = 1024
CAP = 16
POOL = 128
N_CACHE = 4
N_BLK = 4


def paired_draw(key):
    query_key = jax.random.fold_in(key, 101)
    keys_key = jax.random.fold_in(key, 102)
    values_key = jax.random.fold_in(key, 103)
    query_shape = (REQ, SUF, QH * HD)
    half_shape = (REQ, SUF, KVH * HD)
    query_rows = jnp.clip(jax.random.normal(query_key, query_shape, jnp.float32), -6.0, 6.0)
    keys_part = jnp.clip(jax.random.normal(keys_key, half_shape, jnp.float32), -6.0, 6.0)
    values_part = jnp.clip(jax.random.normal(values_key, half_shape, jnp.float32), -6.0, 6.0)
    return (query_rows, jnp.concatenate([keys_part, values_part], axis=-1))


def draw_queries(key, part):
    return paired_draw(key)[0].astype(jnp.bfloat16)


def draw_kv_new(key, part):
    return paired_draw(key)[1].astype(jnp.bfloat16)


def place_ends(drawn, stream_key, least, largest):
    place = [jax.random.randint(jax.random.fold_in(stream_key, axis), (), 0, length) for axis, length in enumerate(drawn.shape)]
    main_axis = drawn.shape.index(max(drawn.shape))
    neighbour = place[:main_axis] + [(place[main_axis] + 1) % drawn.shape[main_axis]] + place[main_axis + 1:]
    return drawn.at[tuple(place)].set(least).at[tuple(neighbour)].set(largest)


def shard_levels(own_key, dims, pieces, smallest, largest):
    level, own = 1.0, jax.random.fold_in(own_key, 6)
    for position, blocks in pieces:
        draws = jnp.exp(jax.random.uniform(jax.random.fold_in(own, position), (blocks,), jnp.float32, smallest / len(pieces), largest / len(pieces)))
        level = level * jnp.repeat(draws, dims[position] // blocks).reshape([-1 if axis == position else 1 for axis in range(len(dims))])
    return level


def split_up(count, total, reach, lean):
    loads = [(1 << 20) // math.isqrt(grade ** lean) + 1 for grade in range(2, count + 1)]
    surplus, given = total - reach - (count - 1), [1] * (count - 1)
    while surplus > 0:
        candidates = [i for i in range(count - 1) if given[i] < reach]
        pool, budget = sum([loads[i] for i in candidates]), surplus
        for i in candidates:
            addition = min(reach - given[i], max(1, budget * loads[i] // pool), surplus)
            given[i] = given[i] + addition
            surplus = surplus - addition
    return np.array([reach] + given)


def ragged_sizes(own_key, count, total, reach, slope):
    if count == 2:
        one = jax.random.randint(own_key, (), max(1, total - reach), min(reach, total - 1) + 1)
        return jnp.stack([one, total - one])
    tallies = jnp.asarray(split_up(count, total, reach, slope), jnp.int32)
    couples = (count - 1) // 2
    donor, receiver = tallies[1:1 + 2 * couples:2], tallies[2:2 + 2 * couples:2]
    margin = jnp.minimum(donor - 1, reach - receiver)
    shifted = jax.random.randint(jax.random.fold_in(own_key, 1), (couples,), 0, 1 << 20) % (margin + 1)
    tallies = tallies.at[1:1 + 2 * couples:2].set(donor - shifted).at[2:2 + 2 * couples:2].set(receiver + shifted)
    return tallies[jax.random.permutation(jax.random.fold_in(own_key, 2), count)]


def shared_out(stream_key, own, number, rows, number_of, top, reach, slope):
    order = jax.random.permutation(stream_key, number_of)
    crowded, ordinary = portions_of(number_of, rows * top, reach, slope, True), portions_of(number_of, rows * top, reach, slope, False)
    places = jnp.arange(number_of)

    def named(sizes, turn):
        used = int((sizes > 0).sum())
        fixed = max(1, used // 4)
        moved = fixed + (places - fixed + turn * (used - fixed)) % max(1, number_of - fixed)
        return jnp.zeros((number_of,), jnp.int32).at[order[jnp.where(places < fixed, places, moved)]].set(jnp.asarray(sizes, jnp.int32))

    sizes = jnp.where(number % 4 == 0, named(crowded, number // 4), named(ordinary, number - number // 4 - 1))
    mixed = jax.random.permutation(jax.random.fold_in(own, 3), number_of)
    giver, receiver = mixed[0:number_of // 2 * 2:2], mixed[1:number_of // 2 * 2:2]
    margin = jnp.minimum(sizes[giver] - 1, reach - sizes[receiver]) // 2
    margin = jnp.where((giver == order[0]) | (receiver == order[0]) | (sizes[receiver] == 0), 0, jnp.maximum(margin, 0))
    moved = jax.random.randint(jax.random.fold_in(own, 4), (number_of // 2,), 0, 1 << 20) % (margin + 1)
    sizes = sizes.at[giver].add(-moved).at[receiver].add(moved)
    labels = jnp.searchsorted(jnp.cumsum(sizes), jnp.arange(rows * top), side="right").astype(jnp.int32)
    grid = labels.reshape(top, rows).T
    grid = grid[jax.random.permutation(jax.random.fold_in(own, 1), rows)]
    turn = jax.random.randint(jax.random.fold_in(own, 2), (rows, 1), 0, top)
    return jnp.take_along_axis(grid, (jnp.arange(top)[None, :] + turn) % top, axis=1)


def portions_of(count, total, bound, skew, full):
    portions = [(1 << 20) // math.isqrt(rank ** skew) + 1 for rank in range(1, count + 1)]
    largest = bound if full else min(bound, max(-(-total // count), total * portions[0] // sum(portions)))
    least = 1 if total - largest >= count - 1 else 0
    given, rest = [largest] + [least] * (count - 1), total - largest - least * (count - 1)
    while rest > 0:
        free = [i for i in range(1, count) if given[i] < largest] or [i for i in range(1, count) if given[i] < bound]
        mass, remaining = sum([portions[i] for i in free]), rest
        for i in free:
            extra = min(bound - given[i], max(1, remaining * portions[i] // mass), rest)
            given[i] = given[i] + extra
            rest = rest - extra
    return np.array(given)


def noise(rng, dims, spread, reach, shards=(), held_as=jnp.bfloat16):
    gain = shard_levels(rng, dims, shards, -0.22, 0.18) if shards else 1.0
    values = jax.random.normal(rng, dims, jnp.float32) * spread * gain
    return jnp.minimum(jnp.maximum(values, -reach), reach).astype(held_as)


def setup_inputs(seed: int = 0, part: int = 0) -> dict:
    key_list = jax.random.split(jax.random.key(seed), 15)
    part_splits = jax.random.split(jax.random.fold_in(key_list[14], part), 15)
    queries = draw_queries(jax.random.fold_in(jax.random.fold_in(key_list[14], part), 71), part)
    kv_new = draw_kv_new(jax.random.fold_in(jax.random.fold_in(key_list[14], part), 71), part)
    page_pool = noise(part_splits[2], (N_CACHE, POOL, PAGE, 2 * KVH * HD), 1.0, 6.0, ((0, 4),))
    page_owner_keys = jax.random.split(jax.random.fold_in(part_splits[3], 1), REQ * N_BLK * LIST // LIST)
    page_owner_turns = jax.random.permutation(jax.random.fold_in(part_splits[3], 3), REQ * N_BLK * LIST // LIST)
    page_owner = jax.vmap(lambda own, number: shared_out(jax.random.fold_in(part_splits[3], 2), own, number, LIST, N_CACHE, 1, CAP, 2))(page_owner_keys, page_owner_turns).reshape((REQ, N_BLK, LIST, 1))
    page_slot = place_ends(jax.random.randint(part_splits[4], (REQ, N_BLK, LIST), 0, POOL), jax.random.fold_in(part_splits[4], 1), 0, POOL - 1).astype(jnp.int32)
    prefix_len = ragged_sizes(part_splits[5], REQ, REQ * PREF // 2, PREF, 2).astype(jnp.int32)
    suffix_len = ragged_sizes(part_splits[6], REQ, REQ * SUF * 3 // 4, SUF, 2).astype(jnp.int32)
    ssm_in = noise(part_splits[7], (REQ, SUF, SH * HP), 1.0, 6.0, ((0, 4), (1, 4)))
    b_in = noise(part_splits[8], (REQ, SUF, NS), 0.25, 4.0, ((0, 4), (1, 4)))
    c_in = noise(part_splits[9], (REQ, SUF, NS), 0.25, 4.0, ((0, 4), (1, 4)))
    step_size = jnp.clip(jnp.exp(math.log(0.1) - 2.3025851 * jax.random.uniform(part_splits[10], (REQ, SUF, SH), jnp.float32) ** shard_levels(part_splits[10], (REQ, SUF, SH), ((0, 4), (1, 4)), -0.2, 0.2)), 0.01, 0.1)
    decay_rate = jnp.clip(jnp.exp(jax.random.uniform(key_list[11], (SH,), jnp.float32, math.log(0.001953125), math.log(4.0))), 0.001953125, 4.0)
    skip_gain = jnp.clip(jax.random.uniform(key_list[12], (SH,), jnp.float32, 0.5, 1.5), 0.5, 1.5)
    prior_state = noise(part_splits[13], (REQ, SH, HP, NS), 0.3, 4.0, ((0, 4),), jnp.float32)
    return dict(queries=queries, kv_new=kv_new, page_pool=page_pool, page_owner=page_owner, page_slot=page_slot, prefix_len=prefix_len, suffix_len=suffix_len, ssm_in=ssm_in, b_in=b_in, c_in=c_in, step_size=step_size, decay_rate=decay_rate, skip_gain=skip_gain, prior_state=prior_state)


NEG = -1e+30

def reference(queries, kv_new, page_pool, page_owner, page_slot, prefix_len, suffix_len, ssm_in, b_in, c_in, step_size, decay_rate, skip_gain, prior_state):
    group = QH // KVH
    kv_half = KVH * HD
    scale = 1.0 / math.sqrt(HD)

    def one_request(packed):
        query_rows, new_rows, owners, slot_rows, prefix_limit, suffix_limit = packed
        pages = page_pool[owners[:, :, 0], slot_rows]
        prefix_rows = jnp.transpose(pages, (1, 0, 2, 3)).reshape(PREF, 2 * kv_half)
        all_rows = jnp.concatenate([prefix_rows, new_rows], axis=0)
        keys_part = all_rows[:, :kv_half].reshape(-1, KVH, HD).astype(jnp.float32)
        values_part = all_rows[:, kv_half:].reshape(-1, KVH, HD).astype(jnp.float32)
        grouped = query_rows.reshape(SUF, KVH, group, HD).astype(jnp.float32)
        scores = jnp.einsum('qhgd,khd->hgqk', grouped, keys_part, precision=lax.Precision.HIGHEST) * scale
        positions = jnp.arange(SUF, dtype=jnp.int32)
        prefix_seen = jnp.broadcast_to((jnp.arange(PREF, dtype=jnp.int32) < prefix_limit)[None, :], (SUF, PREF))
        suffix_seen = (positions[None, :] <= positions[:, None]) & (positions[None, :] < suffix_limit)
        visible = jnp.concatenate([prefix_seen, suffix_seen], axis=1)
        masked = jnp.where(visible[None, None], scores, NEG)
        biggest = lax.optimization_barrier(jnp.max(masked, axis=-1, keepdims=True))
        weights = jnp.where(visible[None, None], jnp.exp(scores - biggest), 0.0)
        totals = lax.optimization_barrier(jnp.sum(weights, axis=-1))
        rounded = lax.optimization_barrier(weights.astype(jnp.bfloat16)).astype(jnp.float32)
        mixed = jnp.einsum('hgqk,khd->hgqd', rounded, values_part, precision=lax.Precision.HIGHEST) / totals[..., None]
        mixed = jnp.transpose(mixed, (2, 0, 1, 3)).reshape(SUF, QH * HD)
        return jnp.where((positions < suffix_limit)[:, None], mixed, 0.0).astype(jnp.bfloat16)
    attn_out = lax.map(one_request, (queries, kv_new, page_owner, page_slot, prefix_len, suffix_len))
    blocks = SUF // SUF_DEV

    def one_sequence(packed):
        inputs, b_rows, c_rows, steps_dt, start_state, suffix_limit = packed
        inputs = inputs.reshape(blocks, SUF_DEV, SH, HP)
        b_rows = b_rows.reshape(blocks, SUF_DEV, NS)
        c_rows = c_rows.reshape(blocks, SUF_DEV, NS)
        steps_dt = steps_dt.reshape(blocks, SUF_DEV, SH)
        positions = jnp.arange(SUF, dtype=jnp.int32).reshape(blocks, SUF_DEV)
        lower = jnp.arange(SUF_DEV)[:, None] >= jnp.arange(SUF_DEV)[None, :]

        def block_step(state, piece):
            block_in, block_b, block_c, block_dt, block_pos = piece
            logs = jnp.cumsum(-block_dt * decay_rate[None, :], axis=0)
            last = logs[-1]
            gram = jnp.dot(block_c, block_b.T, preferred_element_type=jnp.float32)
            exponent = jnp.where(lower[None], logs.T[:, :, None] - logs.T[:, None, :], NEG)
            mixing = gram[None] * jnp.exp(exponent) * block_dt.T[:, None, :]
            mixing = lax.optimization_barrier(mixing.astype(jnp.bfloat16)).astype(jnp.float32)
            wide_in = block_in.astype(jnp.float32)
            inner = jnp.einsum('hts,shp->thp', mixing, wide_in, precision=lax.Precision.HIGHEST)
            scaled = (jnp.exp(last[None, :] - logs) * block_dt)[:, :, None] * wide_in
            scaled = lax.optimization_barrier(scaled.astype(jnp.bfloat16)).astype(jnp.float32)
            local_state = jnp.einsum('shp,sn->hpn', scaled, block_b.astype(jnp.float32), precision=lax.Precision.HIGHEST)
            carried = jnp.exp(logs)[:, :, None] * jnp.einsum('tn,hpn->thp', block_c.astype(jnp.float32), state, precision=lax.Precision.HIGHEST)
            result = inner + carried + skip_gain[None, :, None] * wide_in
            result = jnp.where((block_pos < suffix_limit)[:, None, None], result, 0.0).astype(jnp.bfloat16)
            renewed = jnp.exp(last)[:, None, None] * state + local_state
            return (renewed, result)
        final_state, outputs = lax.scan(block_step, start_state, (inputs, b_rows, c_rows, steps_dt, positions))
        return outputs.reshape(SUF, SH * HP)
    ssm_out = lax.map(one_sequence, (ssm_in, b_in, c_in, step_size, prior_state, suffix_len))
    return (attn_out, ssm_out)
```

```python
import functools
import math

import jax
import jax.numpy as jnp
from jax import lax
from jax.experimental import pallas as pl
from jax.experimental.pallas import tpu as pltpu
from jax.sharding import PartitionSpec as P

QH = 16
KVH = 4
HD = 128
SH = 32
HP = 64
NS = 128
PAGE = 8
GROUP = QH // KVH
NEG = -1e30
CHUNK = 16
F32 = jnp.float32
BF16 = jnp.bfloat16


def remote(src, dst, send_sem, recv_sem, device):
    return pltpu.make_async_remote_copy(
        src_ref=src,
        dst_ref=dst,
        send_sem=send_sem,
        recv_sem=recv_sem,
        device_id=device,
        device_id_type=pl.DeviceIdType.MESH,
    )


def nt(a, b):
    return lax.dot_general(a, b, (((1,), (1,)), ((), ())), preferred_element_type=F32)


def nn(a, b):
    return jnp.dot(a, b, preferred_element_type=F32)


def iota(shape, axis):
    return lax.broadcasted_iota(jnp.int32, shape, axis)


def thirds(v):
    hi = v.astype(BF16).astype(F32)
    rest = v - hi
    mid = rest.astype(BF16).astype(F32)
    return [hi, mid, (rest - mid).astype(BF16).astype(F32)]


def phases_of(total, cap):
    found, done = [], 0
    for have in [cap - CHUNK, cap]:
        if have <= 0:
            continue
        late = total // cap * (cap - have) + max(total % cap - have, 0)
        ready = (total - late) // 16 * 16
        if ready > done:
            found.append((done, ready, have))
            done = ready
    return found


def kernel(
    n, nb, cap, lists, spots,
    plen, slen, owner, slot, q, kv, pool, x_hbm, b_rows, c_rows, dt_t, rate, skip, prior_hbm,
    attn_o, ssm_o,
    code, codes, praw, pf_k, pf_v, pmat, sendbuf, recv, qbuf, kbuf, vbuf, kx, vstage, vt, mbuf, lbuf, accbuf, obuf,
    x, prior, afull, skipf, xp, sbuf, ybuf, hin, hout,
    loc, cs, cr, ps, pr, qs, qr, ks, kr, vs, vr, os, orr, hs, hr,
):
    me = lax.axis_index("cache")
    j = lax.axis_index("blk")
    tok = x.shape[0]
    wide = x.shape[1]
    width = GROUP * HD
    half = KVH * HD
    lanes = code.shape[1]
    rows = GROUP * tok
    prefix_limit = plen[0]
    suffix_limit = slen[0]
    chunks = cap // CHUNK

    def zpeer(d):
        return lax.rem(me + d, n)

    def bpeer(e):
        return lax.rem(j + e, nb)

    def cols(at, size):
        return pl.ds(pl.multiple_of(at, 128), size)

    loads = [
        pltpu.make_async_copy(x_hbm, x, loc.at[0]),
        pltpu.make_async_copy(pool.at[:, cols(j * HD, HD)], praw.at[0], loc.at[1]),
        pltpu.make_async_copy(pool.at[:, cols(half + j * HD, HD)], praw.at[1], loc.at[2]),
        pltpu.make_async_copy(q.at[:, cols(j * width, width)], qbuf.at[j], loc.at[3]),
        pltpu.make_async_copy(kv.at[:, cols(j * HD, HD)], kbuf.at[j], loc.at[4]),
        pltpu.make_async_copy(kv.at[:, cols(half + j * HD, HD)], vbuf.at[j], loc.at[5]),
    ]
    prior_load = pltpu.make_async_copy(prior_hbm, prior, loc.at[6])
    barrier = pltpu.get_barrier_semaphore()

    def greet(k, carry):
        peer = {"cache": zpeer(k // nb), "blk": bpeer(lax.rem(k, nb))}
        pl.semaphore_signal(barrier, inc=1, device_id=peer, device_id_type=pl.DeviceIdType.MESH)
        return carry

    lax.fori_loop(1, n * nb, greet, 0)
    for load in loads:
        load.start()

    @pl.when(j == 0)
    def _():
        prior_load.start()

    mine = iota((1, lanes), 1) // lists == j
    code[...] = jnp.zeros_like(code)
    code[0:1, :] = jnp.where(mine, jnp.concatenate([owner[...]] * nb, axis=1) + 1, 0)
    code[1:2, :] = jnp.where(mine, jnp.concatenate([slot[...]] * nb, axis=1), 0)
    codes[me, j] = code[...]

    dt = dt_t[...].T
    fall = jnp.concatenate(thirds(dt * (-rate[...])), axis=0).astype(BF16)
    tri = jnp.where(iota((tok, 3 * tok), 0) >= lax.rem(iota((tok, 3 * tok), 1), tok), 1.0, 0.0).astype(BF16)
    logs = nn(tri, fall)
    gains = jnp.concatenate([jnp.exp(logs), jnp.broadcast_to(skip[...], (16, SH))], axis=0)
    a3 = jnp.concatenate(thirds(gains), axis=1).astype(BF16)
    b3 = jnp.concatenate(thirds(jnp.exp(-logs) * dt), axis=1).astype(BF16)
    lower = iota((tok, tok), 0) >= iota((tok, tok), 1)
    gram = jnp.where(lower, nt(c_rows[...], b_rows[...]), 0.0).astype(BF16)
    readout = jnp.concatenate([gram, c_rows[...]], axis=1)
    b_t = b_rows[...].astype(F32).T.astype(BF16)
    part = 2 * HD
    parts = wide // part

    loads[0].wait()

    def own_block(i, carry):
        at = cols(i * part, part)
        heads = lax.rem(iota((3 * SH, part), 0), SH)
        spread = jnp.where(heads == iota((3 * SH, part), 1) // HP + i * (part // HP), 1.0, 0.0).astype(BF16)
        grown = nn(a3, spread)
        afull[:, at] = grown[0:tok]
        skipf[:, at] = grown[tok : tok + 8]
        scaled = (nn(b3, spread) * x[:, at].astype(F32)).astype(BF16)
        xp[:, at] = scaled
        sbuf[:, at] = nn(b_t, scaled)
        return carry

    lax.fori_loop(0, parts, own_block, 0)

    def onward(i, carry):
        at = cols(i * part, part)
        hout[:, at] = (afull[tok - 1 : tok, at] * (hin[:, at].astype(F32) + sbuf[:, at])).astype(BF16)
        return carry

    @pl.when(j == 0)
    def _():
        prior_load.wait()

        def fill(i, carry):
            at = cols(i * HD, HD)
            hin[:, at] = prior[at, :].T.astype(BF16)
            return carry

        lax.fori_loop(0, wide // HD, fill, 0)
        lax.fori_loop(0, parts, onward, 0)

    loads[1].wait()
    loads[2].wait()
    pf_k[...] = praw[0].astype(F32)
    pf_v[...] = praw[1].astype(F32)
    if spots < pmat.shape[0]:
        pmat[...] = jnp.zeros_like(pmat)
    for i in range(PAGE):
        at = pl.ds(i, spots, stride=PAGE)
        pmat[0:spots, i * HD : (i + 1) * HD] = pf_k[at, :].astype(BF16)
        pmat[0:spots, (PAGE + i) * HD : (PAGE + i + 1) * HD] = pf_v[at, :].astype(BF16)

    pl.semaphore_wait(barrier, n * nb - 1)

    def code_copy(k):
        peer = {"cache": zpeer(k // nb), "blk": bpeer(lax.rem(k, nb))}
        return remote(code, codes.at[me, j], cs.at[k], cr.at[k], peer)

    def q_copy(e):
        to = bpeer(e)
        return remote(q.at[:, cols(to * width, width)], qbuf.at[j], qs.at[e], qr.at[e], {"blk": to})

    def k_copy(e):
        to = bpeer(e)
        return remote(kv.at[:, cols(to * HD, HD)], kbuf.at[j], ks.at[e], kr.at[e], {"blk": to})

    def v_copy(e):
        to = bpeer(e)
        return remote(kv.at[:, cols(half + to * HD, HD)], vbuf.at[j], vs.at[e], vr.at[e], {"blk": to})

    def page_copy(d, c):
        at = pl.ds(c * CHUNK, CHUNK)
        return remote(sendbuf.at[d, at], recv.at[d, at], ps.at[d, c], pr.at[d, c], {"cache": zpeer(d)})

    def state_copy():
        return remote(hout, hin, hs, hr, {"blk": bpeer(1)})

    def out_copy(e):
        to = bpeer(e)
        return remote(obuf.at[to], attn_o.at[:, cols(j * width, width)], os.at[e], orr.at[e], {"blk": to})

    def each(what, low, high):
        if high - low <= 4:
            for i in range(low, high):
                what(i)
            return

        def body(i, carry):
            what(i)
            return carry

        lax.fori_loop(low, high, body, 0)

    def each_code(what):
        def body(k, carry):
            what(k)
            return carry

        lax.fori_loop(1, n * nb, body, 0)

    each_code(lambda k: code_copy(k).start())

    @pl.when(j == 0)
    def _():
        state_copy().start()

    each(lambda e: (k_copy(e).start(), v_copy(e).start(), q_copy(e).start()), 1, nb)

    before = jnp.where(iota((lanes, lanes), 0) < iota((lanes, lanes), 1), 1.0, 0.0).astype(BF16)

    def comb(r):
        return jnp.sum(codes[r], axis=0)

    def ranked(named):
        flags = jnp.broadcast_to(jnp.where(named, 1.0, 0.0), (16, lanes)).astype(BF16)
        return nn(flags, before)[0:1].astype(jnp.int32)

    def onehot(flag):
        return jnp.where(flag, 1.0, 0.0).astype(BF16)

    each_code(lambda k: code_copy(k).wait_recv())
    spread_spots = pmat.shape[0]

    def answer(d):
        pair = comb(zpeer(d))
        named = pair[0:1] == me + 1
        place = onehot((ranked(named) == iota((cap, lanes), 0)) & named)
        wants = onehot(pair[1:2] == iota((spread_spots, lanes), 0))
        chosen = nt(place, wants).astype(BF16)
        for i in range(2 * PAGE * HD // part):
            sendbuf[d, :, i * part : (i + 1) * part] = nn(chosen, pmat[:, i * part : (i + 1) * part]).astype(BF16)
        page_copy(d, 0).start()

    each(answer, 1, n)
    for c in range(1, chunks):
        each(lambda d: page_copy(d, c).start(), 1, n)

    pair = comb(me)
    back = me + 1 - pair[0:1]
    away = jnp.where(back < 0, back + n, back)
    rank = jnp.zeros((1, lanes), jnp.int32)

    def add_rank(d, rank):
        named = away == d
        return rank + jnp.where(named, ranked(named), 0)

    if n <= 8:
        for d in range(1, n):
            rank = add_rank(d, rank)
    else:
        rank = lax.fori_loop(1, n, add_rank, rank)
    lane = iota((1, lanes), 1)
    turn = jnp.where(away == 0, 0, rank // CHUNK) * lanes + lane
    turn_f = turn.astype(F32)
    turn_col = jnp.broadcast_to(turn_f, (lanes, lanes)).T
    ahead = jnp.where(turn_col < turn_f, 1.0, 0.0)
    spot = jnp.sum(ahead, axis=0, keepdims=True).astype(jnp.int32)
    sorted_f = jnp.where(iota((lanes, lanes), 0) == spot, 1.0, 0.0)
    sorting = sorted_f.astype(BF16)
    number = (lax.rem(lane, lists) * nb + lane // lists).astype(F32)
    first_row = jnp.sum(sorted_f * number, axis=1, keepdims=True).astype(jnp.int32) * PAGE
    own_wants = onehot((pair[1:2] == iota((spread_spots, lanes), 0)) & (away == 0))
    places = [onehot((rank == iota((cap, lanes), 0)) & (away == d)) for d in range(1, n)]

    def read_block():
        alive = j * tok + iota((tok, part), 0) < suffix_limit

        def body(i, carry):
            at = cols(i * part, part)
            both = jnp.concatenate([xp[:, at], hin[:, at]], axis=0)
            total = afull[:, at] * nn(readout, both) + skipf[0:1, at] * x[:, at].astype(F32)
            ybuf[:, at] = jnp.where(alive, total, 0.0).astype(BF16)
            return carry

        lax.fori_loop(0, parts, body, 0)

    def chain():
        state_copy().wait_recv()

        @pl.when(j < nb - 1)
        def _():
            lax.fori_loop(0, parts, onward, 0)
            state_copy().start()

        read_block()

    pl.when(j == 0)(read_block)
    pl.when(j == 1)(chain)

    rate2 = math.log2(math.e) / math.sqrt(HD)
    first_lane = iota((1, HD), 1) == 0
    one_column = jnp.broadcast_to(jnp.where(first_lane, 1.0, 0.0), (tok, HD)).astype(BF16)

    def queries(b):
        pieces = [jnp.concatenate([qbuf[b, :, h * HD : (h + 1) * HD], one_column], axis=1) for h in range(GROUP)]
        return jnp.concatenate(pieces, axis=0)

    def bias(visible, size):
        column = jnp.where(visible, 0.0, NEG)
        return jnp.where(first_lane, jnp.broadcast_to(column, (size, HD)), 0.0).astype(BF16)

    for load in loads[3:]:
        load.wait()
    each(lambda e: (k_copy(e).wait_recv(), v_copy(e).wait_recv(), q_copy(e).wait_recv()), 1, nb)

    for b in range(nb):
        kx[b * tok : (b + 1) * tok, 0:HD] = kbuf[b]
        kx[b * tok : (b + 1) * tok, HD : 2 * HD] = bias(b * tok + iota((tok, 1), 0) < suffix_limit, tok)
        vt[:, b * tok : (b + 1) * tok] = vbuf[b].astype(F32).T.astype(BF16)
    causal = jnp.where(iota((tok, rows), 0) <= lax.rem(iota((tok, rows), 1), tok), 0.0, NEG)
    for b in range(nb):
        count = (b + 1) * tok
        qb = queries(b)
        scores = nt(kx[0:count, :], qb)
        near = scores[count - tok :] + causal
        scores = near if b == 0 else jnp.concatenate([scores[: count - tok], near], axis=0)
        top = jnp.max(scores, axis=0, keepdims=True) * rate2
        weights = jnp.exp2(scores * rate2 - top)
        mbuf[b] = top
        lbuf[b] = jnp.sum(weights, axis=0, keepdims=True)
        accbuf[b] = nn(vt[:, 0:count], weights.astype(BF16))

    pl.when(j >= 2)(chain)
    ssm_store = pltpu.make_async_copy(ybuf, ssm_o, loc.at[7])
    ssm_store.start()

    phases = phases_of(lanes, cap)
    arrived = 0
    for low, high, have in phases:
        last = high == lanes
        for c in range(arrived, have // CHUNK):
            each(lambda d: page_copy(d, c).wait_recv(), 1, n)
        arrived = have // CHUNK
        pages = high - low
        table = jnp.concatenate([own_wants] + [p[0:have] for p in places], axis=0)
        pick = nt(sorting[low:high], table).astype(BF16)
        for i in range(2 * PAGE * HD // part):
            at = slice(i * part, (i + 1) * part)
            got = recv[1:n, 0:have, at].reshape((n - 1) * have, part)
            out = nn(pick, jnp.concatenate([pmat[:, at], got], axis=0))
            for k in range(2):
                row = 2 * i + k
                piece = out[:, k * HD : (k + 1) * HD]
                if row < PAGE:
                    kx[row * pages : (row + 1) * pages, 0:HD] = piece.astype(BF16)
                    kx[row * pages : (row + 1) * pages, HD : 2 * HD] = bias(first_row[low:high] + row < prefix_limit, pages)
                else:
                    vstage[(row - PAGE) * pages : (row - PAGE + 1) * pages, :] = piece
        count = PAGE * pages
        for i in range(count // HD):
            vt[:, i * HD : (i + 1) * HD] = vstage[i * HD : (i + 1) * HD, :].T.astype(BF16)

        def block(e, carry, count=count, last=last):
            b = bpeer(e)
            scores = nt(kx[0:count, :], queries(b))
            old = mbuf[b]
            top = jnp.maximum(jnp.max(scores, axis=0, keepdims=True) * rate2, old)
            weights = jnp.exp2(scores * rate2 - top)
            factor = jnp.exp2(old - top)
            total = jnp.sum(weights, axis=0, keepdims=True) + lbuf[b] * factor
            mixed = nn(vt[:, 0:count], weights.astype(BF16)) + accbuf[b] * factor
            if not last:
                mbuf[b] = top
                lbuf[b] = total
                accbuf[b] = mixed
            else:
                alive = b * tok + lax.rem(iota((1, rows), 1), tok) < suffix_limit
                final = mixed * jnp.where(alive, 1.0 / total, 0.0)
                for h in range(GROUP):
                    obuf[b, :, h * HD : (h + 1) * HD] = final[:, h * tok : (h + 1) * tok].T.astype(BF16)

                @pl.when(e < nb)
                def _():
                    out_copy(e).start()
            return carry

        lax.fori_loop(1, nb + 1, block, 0)

    own_store = pltpu.make_async_copy(obuf.at[j], attn_o.at[:, cols(j * width, width)], loc.at[8])
    own_store.start()
    each_code(lambda k: code_copy(k).wait_send())
    each(lambda e: (q_copy(e).wait_send(), k_copy(e).wait_send(), v_copy(e).wait_send()), 1, nb)
    for c in range(chunks):
        each(lambda d: page_copy(d, c).wait_send(), 1, n)

    @pl.when(j < nb - 1)
    def _():
        state_copy().wait_send()

    ssm_store.wait()
    own_store.wait()
    each(lambda e: out_copy(e).wait(), 1, nb)


def hand_over(attn_i, ssm_i, attn_o, ssm_o, sems):
    pieces = sems.shape[0] // 2
    size = attn_i.shape[0] // pieces
    copies = []
    for k, (src, dst) in enumerate([(attn_i, attn_o), (ssm_i, ssm_o)]):
        for p in range(pieces):
            at = pl.ds(p * size, size)
            copies.append(pltpu.make_async_copy(src.at[at], dst.at[at], sems.at[k * pieces + p]))
    for copy in copies:
        copy.start()
    for copy in copies:
        copy.wait()


def local(
    queries, kv_new, page_pool, page_owner, page_slot, prefix_len, suffix_len,
    ssm_in, b_in, c_in, step_size, decay_rate, skip_gain, prior_state,
):
    n = lax.axis_size("cache")
    nb = lax.axis_size("blk")
    tok = queries.shape[1]
    lists = page_owner.shape[2]
    lanes = nb * lists
    cap = max(16, max(2, 2 * lists // n) * nb)
    spots = page_pool.shape[1]
    spread_spots = max(spots, 128)
    vmem = pl.BlockSpec(memory_space=pltpu.VMEM)
    smem = pl.BlockSpec(memory_space=pltpu.SMEM)
    hbm = pl.BlockSpec(memory_space=pl.ANY)
    dma = pltpu.SemaphoreType.DMA
    wide = SH * HP
    rows = GROUP * tok
    most = max([nb * tok] + [PAGE * (high - low) for low, high, _ in phases_of(lanes, cap)])
    chunks = cap // CHUNK
    results = (
        jax.ShapeDtypeStruct((tok, QH * HD), BF16),
        jax.ShapeDtypeStruct((tok, wide), BF16),
    )
    attn, ssm = pl.pallas_call(
        functools.partial(kernel, n, nb, cap, lists, spots),
        out_shape=results,
        in_specs=[smem, smem, vmem, vmem, hbm, hbm, hbm, hbm, vmem, vmem, vmem, vmem, vmem, hbm],
        out_specs=(hbm, hbm),
        scratch_shapes=[
            pltpu.VMEM((8, lanes), jnp.int32),
            pltpu.VMEM((n, nb, 8, lanes), jnp.int32),
            pltpu.VMEM((2, spots * PAGE, HD), BF16),
            pltpu.VMEM((spots * PAGE, HD), F32),
            pltpu.VMEM((spots * PAGE, HD), F32),
            pltpu.VMEM((spread_spots, 2 * PAGE * HD), BF16),
            pltpu.VMEM((n, cap, 2 * PAGE * HD), BF16),
            pltpu.VMEM((n, cap, 2 * PAGE * HD), BF16),
            pltpu.VMEM((nb, tok, GROUP * HD), BF16),
            pltpu.VMEM((nb, tok, HD), BF16),
            pltpu.VMEM((nb, tok, HD), BF16),
            pltpu.VMEM((most, 2 * HD), BF16),
            pltpu.VMEM((most, HD), F32),
            pltpu.VMEM((HD, most), BF16),
            pltpu.VMEM((nb, 1, rows), F32),
            pltpu.VMEM((nb, 1, rows), F32),
            pltpu.VMEM((nb, HD, rows), F32),
            pltpu.VMEM((nb, tok, GROUP * HD), BF16),
            pltpu.VMEM((tok, wide), BF16),
            pltpu.VMEM((wide, NS), F32),
            pltpu.VMEM((tok, wide), F32),
            pltpu.VMEM((8, wide), F32),
            pltpu.VMEM((tok, wide), BF16),
            pltpu.VMEM((NS, wide), F32),
            pltpu.VMEM((tok, wide), BF16),
            pltpu.VMEM((NS, wide), BF16),
            pltpu.VMEM((NS, wide), BF16),
            dma((9,)), dma((n * nb,)), dma((n * nb,)), dma((n, chunks)), dma((n, chunks)),
            dma((nb,)), dma((nb,)), dma((nb,)), dma((nb,)), dma((nb,)), dma((nb,)),
            dma((nb,)), dma((nb,)), dma, dma,
        ],
        compiler_params=pltpu.CompilerParams(
            collective_id=0, has_side_effects=True, vmem_limit_bytes=56 * 1024 * 1024
        ),
    )(
        prefix_len, suffix_len, page_owner[0, 0, :, 0][None], page_slot[0], queries[0], kv_new[0],
        page_pool.reshape(spots * PAGE, 2 * KVH * HD), ssm_in[0], b_in[0], c_in[0], step_size[0].T,
        decay_rate[None, :], skip_gain[None, :], prior_state.reshape(wide, NS),
    )
    attn, ssm = pl.pallas_call(
        hand_over,
        out_shape=results,
        in_specs=[hbm, hbm],
        out_specs=(hbm, hbm),
        scratch_shapes=[dma((8,))],
    )(attn, ssm)
    return attn[None], ssm[None]


def solution(mesh):
    in_specs = (
        P(("groups", "cache"), "blk", None),
        P(("groups", "cache"), "blk", None),
        P(("groups", "cache"), None, None, None),
        P(("groups", "cache"), "blk", None, None),
        P(("groups", "cache"), "blk", None),
        P(("groups", "cache")),
        P(("groups", "cache")),
        P(("groups", "cache"), "blk", None),
        P(("groups", "cache"), "blk", None),
        P(("groups", "cache"), "blk", None),
        P(("groups", "cache"), "blk", None),
        P(),
        P(),
        P(("groups", "cache"), None, None, None),
    )
    out_specs = (P(("groups", "cache"), "blk", None), P(("groups", "cache"), "blk", None))
    return jax.shard_map(local, mesh=mesh, in_specs=in_specs, out_specs=out_specs, check_vma=False)
```

```python
import functools
import math

import jax
import jax.numpy as jnp
from jax import lax
from jax.experimental import pallas as pl
from jax.experimental.pallas import tpu as pltpu
from jax.sharding import PartitionSpec as P

QH = 16
KVH = 4
HD = 128
SH = 32
HP = 64
NS = 128
PAGE = 8
GROUP = QH // KVH
NEG = -1e30
CHUNK = 16
F32 = jnp.float32
BF16 = jnp.bfloat16


def remote(src, dst, send_sem, recv_sem, device):
    return pltpu.make_async_remote_copy(
        src_ref=src,
        dst_ref=dst,
        send_sem=send_sem,
        recv_sem=recv_sem,
        device_id=device,
        device_id_type=pl.DeviceIdType.MESH,
    )


def nt(a, b):
    return lax.dot_general(a, b, (((1,), (1,)), ((), ())), preferred_element_type=F32)


def nn(a, b):
    return jnp.dot(a, b, preferred_element_type=F32)


def iota(shape, axis):
    return lax.broadcasted_iota(jnp.int32, shape, axis)


def thirds(v):
    hi = v.astype(BF16).astype(F32)
    rest = v - hi
    mid = rest.astype(BF16).astype(F32)
    return [hi, mid, (rest - mid).astype(BF16).astype(F32)]


def phases_of(total, cap):
    found, done = [], 0
    for have in [cap - CHUNK, cap]:
        if have <= 0:
            continue
        late = total // cap * (cap - have) + max(total % cap - have, 0)
        ready = (total - late) // 16 * 16
        if ready > done:
            found.append((done, ready, have))
            done = ready
    return found


def kernel(
    n, nb, cap, lists, spots,
    plen, slen, owner, slot, q, kv, pool, x_hbm, b_rows, c_rows, dt_t, rate, skip, prior_hbm,
    attn_o, ssm_o,
    code, codes, praw, pf_k, pf_v, pmat, sendbuf, recv, qbuf, kbuf, vbuf, kx, vstage, vt, mbuf, lbuf, accbuf, obuf,
    x, prior, afull, skipf, xp, sbuf, ybuf, hin, hout,
    loc, cs, cr, ps, pr, qs, qr, ks, kr, vs, vr, os, orr, hs, hr,
):
    me = lax.axis_index("cache")
    j = lax.axis_index("blk")
    tok = x.shape[0]
    wide = x.shape[1]
    width = GROUP * HD
    half = KVH * HD
    lanes = code.shape[1]
    rows = GROUP * tok
    prefix_limit = plen[0]
    suffix_limit = slen[0]
    chunks = cap // CHUNK

    def zpeer(d):
        return lax.rem(me + d, n)

    def bpeer(e):
        return lax.rem(j + e, nb)

    def cols(at, size):
        return pl.ds(pl.multiple_of(at, 128), size)

    loads = [
        pltpu.make_async_copy(x_hbm, x, loc.at[0]),
        pltpu.make_async_copy(pool.at[:, cols(j * HD, HD)], praw.at[0], loc.at[1]),
        pltpu.make_async_copy(pool.at[:, cols(half + j * HD, HD)], praw.at[1], loc.at[2]),
        pltpu.make_async_copy(q.at[:, cols(j * width, width)], qbuf.at[j], loc.at[3]),
        pltpu.make_async_copy(kv.at[:, cols(j * HD, HD)], kbuf.at[j], loc.at[4]),
        pltpu.make_async_copy(kv.at[:, cols(half + j * HD, HD)], vbuf.at[j], loc.at[5]),
    ]
    prior_load = pltpu.make_async_copy(prior_hbm, prior, loc.at[6])
    barrier = pltpu.get_barrier_semaphore()

    def greet(k, carry):
        peer = {"cache": zpeer(k // nb), "blk": bpeer(lax.rem(k, nb))}
        pl.semaphore_signal(barrier, inc=1, device_id=peer, device_id_type=pl.DeviceIdType.MESH)
        return carry

    lax.fori_loop(1, n * nb, greet, 0)
    for load in loads:
        load.start()

    @pl.when(j == 0)
    def _():
        prior_load.start()

    mine = iota((1, lanes), 1) // lists == j
    code[...] = jnp.zeros_like(code)
    code[0:1, :] = jnp.where(mine, jnp.concatenate([owner[...]] * nb, axis=1) + 1, 0)
    code[1:2, :] = jnp.where(mine, jnp.concatenate([slot[...]] * nb, axis=1), 0)
    codes[me, j] = code[...]

    dt = dt_t[...].T
    fall = jnp.concatenate(thirds(dt * (-rate[...])), axis=0).astype(BF16)
    tri = jnp.where(iota((tok, 3 * tok), 0) >= lax.rem(iota((tok, 3 * tok), 1), tok), 1.0, 0.0).astype(BF16)
    logs = nn(tri, fall)
    gains = jnp.concatenate([jnp.exp(logs), jnp.broadcast_to(skip[...], (16, SH))], axis=0)
    a3 = jnp.concatenate(thirds(gains), axis=1).astype(BF16)
    b3 = jnp.concatenate(thirds(jnp.exp(-logs) * dt), axis=1).astype(BF16)
    lower = iota((tok, tok), 0) >= iota((tok, tok), 1)
    gram = jnp.where(lower, nt(c_rows[...], b_rows[...]), 0.0).astype(BF16)
    readout = jnp.concatenate([gram, c_rows[...]], axis=1)
    b_t = b_rows[...].astype(F32).T.astype(BF16)
    part = 2 * HD
    parts = wide // part

    loads[0].wait()

    def own_block(i, carry):
        at = cols(i * part, part)
        heads = lax.rem(iota((3 * SH, part), 0), SH)
        spread = jnp.where(heads == iota((3 * SH, part), 1) // HP + i * (part // HP), 1.0, 0.0).astype(BF16)
        grown = nn(a3, spread)
        afull[:, at] = grown[0:tok]
        skipf[:, at] = grown[tok : tok + 8]
        scaled = (nn(b3, spread) * x[:, at].astype(F32)).astype(BF16)
        xp[:, at] = scaled
        sbuf[:, at] = nn(b_t, scaled)
        return carry

    lax.fori_loop(0, parts, own_block, 0)

    def onward(i, carry):
        at = cols(i * part, part)
        hout[:, at] = (afull[tok - 1 : tok, at] * (hin[:, at].astype(F32) + sbuf[:, at])).astype(BF16)
        return carry

    @pl.when(j == 0)
    def _():
        prior_load.wait()

        def fill(i, carry):
            at = cols(i * HD, HD)
            hin[:, at] = prior[at, :].T.astype(BF16)
            return carry

        lax.fori_loop(0, wide // HD, fill, 0)
        lax.fori_loop(0, parts, onward, 0)

    loads[1].wait()
    loads[2].wait()
    pf_k[...] = praw[0].astype(F32)
    pf_v[...] = praw[1].astype(F32)
    if spots < pmat.shape[0]:
        pmat[...] = jnp.zeros_like(pmat)
    for i in range(PAGE):
        at = pl.ds(i, spots, stride=PAGE)
        pmat[0:spots, i * HD : (i + 1) * HD] = pf_k[at, :].astype(BF16)
        pmat[0:spots, (PAGE + i) * HD : (PAGE + i + 1) * HD] = pf_v[at, :].astype(BF16)

    pl.semaphore_wait(barrier, n * nb - 1)

    def code_copy(k):
        peer = {"cache": zpeer(k // nb), "blk": bpeer(lax.rem(k, nb))}
        return remote(code, codes.at[me, j], cs.at[k], cr.at[k], peer)

    def q_copy(e):
        to = bpeer(e)
        return remote(q.at[:, cols(to * width, width)], qbuf.at[j], qs.at[e], qr.at[e], {"blk": to})

    def k_copy(e):
        to = bpeer(e)
        return remote(kv.at[:, cols(to * HD, HD)], kbuf.at[j], ks.at[e], kr.at[e], {"blk": to})

    def v_copy(e):
        to = bpeer(e)
        return remote(kv.at[:, cols(half + to * HD, HD)], vbuf.at[j], vs.at[e], vr.at[e], {"blk": to})

    def page_copy(d, c):
        at = pl.ds(c * CHUNK, CHUNK)
        return remote(sendbuf.at[d, at], recv.at[d, at], ps.at[d, c], pr.at[d, c], {"cache": zpeer(d)})

    def state_copy():
        return remote(hout, hin, hs, hr, {"blk": bpeer(1)})

    def out_copy(e):
        to = bpeer(e)
        return remote(obuf.at[to], attn_o.at[:, cols(j * width, width)], os.at[e], orr.at[e], {"blk": to})

    def each(what, low, high):
        if high - low <= 4:
            for i in range(low, high):
                what(i)
            return

        def body(i, carry):
            what(i)
            return carry

        lax.fori_loop(low, high, body, 0)

    def each_code(what):
        def body(k, carry):
            what(k)
            return carry

        lax.fori_loop(1, n * nb, body, 0)

    each_code(lambda k: code_copy(k).start())

    @pl.when(j == 0)
    def _():
        state_copy().start()

    each(lambda e: (k_copy(e).start(), v_copy(e).start(), q_copy(e).start()), 1, nb)

    before = jnp.where(iota((lanes, lanes), 0) < iota((lanes, lanes), 1), 1.0, 0.0).astype(BF16)

    def comb(r):
        return jnp.sum(codes[r], axis=0)

    def ranked(named):
        flags = jnp.broadcast_to(jnp.where(named, 1.0, 0.0), (16, lanes)).astype(BF16)
        return nn(flags, before)[0:1].astype(jnp.int32)

    def onehot(flag):
        return jnp.where(flag, 1.0, 0.0).astype(BF16)

    each_code(lambda k: code_copy(k).wait_recv())
    spread_spots = pmat.shape[0]

    def answer(d):
        pair = comb(zpeer(d))
        named = pair[0:1] == me + 1
        place = onehot((ranked(named) == iota((cap, lanes), 0)) & named)
        wants = onehot(pair[1:2] == iota((spread_spots, lanes), 0))
        chosen = nt(place, wants).astype(BF16)
        for i in range(2 * PAGE * HD // part):
            sendbuf[d, :, i * part : (i + 1) * part] = nn(chosen, pmat[:, i * part : (i + 1) * part]).astype(BF16)
        page_copy(d, 0).start()

    each(answer, 1, n)
    for c in range(1, chunks):
        each(lambda d: page_copy(d, c).start(), 1, n)

    pair = comb(me)
    back = me + 1 - pair[0:1]
    away = jnp.where(back < 0, back + n, back)
    rank = jnp.zeros((1, lanes), jnp.int32)

    def add_rank(d, rank):
        named = away == d
        return rank + jnp.where(named, ranked(named), 0)

    if n <= 8:
        for d in range(1, n):
            rank = add_rank(d, rank)
    else:
        rank = lax.fori_loop(1, n, add_rank, rank)
    lane = iota((1, lanes), 1)
    turn = jnp.where(away == 0, 0, rank // CHUNK) * lanes + lane
    turn_f = turn.astype(F32)
    turn_col = jnp.broadcast_to(turn_f, (lanes, lanes)).T
    ahead = jnp.where(turn_col < turn_f, 1.0, 0.0)
    spot = jnp.sum(ahead, axis=0, keepdims=True).astype(jnp.int32)
    sorted_f = jnp.where(iota((lanes, lanes), 0) == spot, 1.0, 0.0)
    sorting = sorted_f.astype(BF16)
    number = (lax.rem(lane, lists) * nb + lane // lists).astype(F32)
    first_row = jnp.sum(sorted_f * number, axis=1, keepdims=True).astype(jnp.int32) * PAGE
    own_wants = onehot((pair[1:2] == iota((spread_spots, lanes), 0)) & (away == 0))
    places = [onehot((rank == iota((cap, lanes), 0)) & (away == d)) for d in range(1, n)]

    def read_block():
        alive = j * tok + iota((tok, part), 0) < suffix_limit

        def body(i, carry):
            at = cols(i * part, part)
            both = jnp.concatenate([xp[:, at], hin[:, at]], axis=0)
            total = afull[:, at] * nn(readout, both) + skipf[0:1, at] * x[:, at].astype(F32)
            ybuf[:, at] = jnp.where(alive, total, 0.0).astype(BF16)
            return carry

        lax.fori_loop(0, parts, body, 0)

    def chain():
        state_copy().wait_recv()

        @pl.when(j < nb - 1)
        def _():
            lax.fori_loop(0, parts, onward, 0)
            state_copy().start()

        read_block()

    pl.when(j == 0)(read_block)
    pl.when(j == 1)(chain)

    rate2 = math.log2(math.e) / math.sqrt(HD)
    first_lane = iota((1, HD), 1) == 0
    one_column = jnp.broadcast_to(jnp.where(first_lane, 1.0, 0.0), (tok, HD)).astype(BF16)

    def queries(b):
        pieces = [jnp.concatenate([qbuf[b, :, h * HD : (h + 1) * HD], one_column], axis=1) for h in range(GROUP)]
        return jnp.concatenate(pieces, axis=0)

    def bias(visible, size):
        column = jnp.where(visible, 0.0, NEG)
        return jnp.where(first_lane, jnp.broadcast_to(column, (size, HD)), 0.0).astype(BF16)

    for load in loads[3:]:
        load.wait()
    each(lambda e: (k_copy(e).wait_recv(), v_copy(e).wait_recv(), q_copy(e).wait_recv()), 1, nb)

    for b in range(nb):
        kx[b * tok : (b + 1) * tok, 0:HD] = kbuf[b]
        kx[b * tok : (b + 1) * tok, HD : 2 * HD] = bias(b * tok + iota((tok, 1), 0) < suffix_limit, tok)
        vt[:, b * tok : (b + 1) * tok] = vbuf[b].astype(F32).T.astype(BF16)
    causal = jnp.where(iota((tok, rows), 0) <= lax.rem(iota((tok, rows), 1), tok), 0.0, NEG)
    for b in range(nb):
        count = (b + 1) * tok
        qb = queries(b)
        scores = nt(kx[0:count, :], qb)
        near = scores[count - tok :] + causal
        scores = near if b == 0 else jnp.concatenate([scores[: count - tok], near], axis=0)
        top = jnp.max(scores, axis=0, keepdims=True) * rate2
        weights = jnp.exp2(scores * rate2 - top)
        mbuf[b] = top
        lbuf[b] = jnp.sum(weights, axis=0, keepdims=True)
        accbuf[b] = nn(vt[:, 0:count], weights.astype(BF16))

    pl.when(j >= 2)(chain)
    ssm_store = pltpu.make_async_copy(ybuf, ssm_o, loc.at[7])
    ssm_store.start()

    phases = phases_of(lanes, cap)
    arrived = 0
    for low, high, have in phases:
        last = high == lanes
        for c in range(arrived, have // CHUNK):
            each(lambda d: page_copy(d, c).wait_recv(), 1, n)
        arrived = have // CHUNK
        pages = high - low
        table = jnp.concatenate([own_wants] + [p[0:have] for p in places], axis=0)
        pick = nt(sorting[low:high], table).astype(BF16)
        for i in range(2 * PAGE * HD // part):
            at = slice(i * part, (i + 1) * part)
            got = recv[1:n, 0:have, at].reshape((n - 1) * have, part)
            out = nn(pick, jnp.concatenate([pmat[:, at], got], axis=0))
            for k in range(2):
                row = 2 * i + k
                piece = out[:, k * HD : (k + 1) * HD]
                if row < PAGE:
                    kx[row * pages : (row + 1) * pages, 0:HD] = piece.astype(BF16)
                    kx[row * pages : (row + 1) * pages, HD : 2 * HD] = bias(first_row[low:high] + row < prefix_limit, pages)
                else:
                    vstage[(row - PAGE) * pages : (row - PAGE + 1) * pages, :] = piece
        count = PAGE * pages
        for i in range(count // HD):
            vt[:, i * HD : (i + 1) * HD] = vstage[i * HD : (i + 1) * HD, :].T.astype(BF16)

        def block(e, carry, count=count, last=last):
            b = bpeer(e)
            scores = nt(kx[0:count, :], queries(b))
            old = mbuf[b]
            top = jnp.maximum(jnp.max(scores, axis=0, keepdims=True) * rate2, old)
            weights = jnp.exp2(scores * rate2 - top)
            factor = jnp.exp2(old - top)
            total = jnp.sum(weights, axis=0, keepdims=True) + lbuf[b] * factor
            mixed = nn(vt[:, 0:count], weights.astype(BF16)) + accbuf[b] * factor
            if not last:
                mbuf[b] = top
                lbuf[b] = total
                accbuf[b] = mixed
            else:
                alive = b * tok + lax.rem(iota((1, rows), 1), tok) < suffix_limit
                final = mixed * jnp.where(alive, 1.0 / total, 0.0)
                for h in range(GROUP):
                    obuf[b, :, h * HD : (h + 1) * HD] = final[:, h * tok : (h + 1) * tok].T.astype(BF16)

                @pl.when(e < nb)
                def _():
                    out_copy(e).start()
            return carry

        lax.fori_loop(1, nb + 1, block, 0)

    own_store = pltpu.make_async_copy(obuf.at[j], attn_o.at[:, cols(j * width, width)], loc.at[8])
    own_store.start()
    each_code(lambda k: code_copy(k).wait_send())
    each(lambda e: (q_copy(e).wait_send(), k_copy(e).wait_send(), v_copy(e).wait_send()), 1, nb)
    for c in range(chunks):
        each(lambda d: page_copy(d, c).wait_send(), 1, n)

    @pl.when(j < nb - 1)
    def _():
        state_copy().wait_send()

    ssm_store.wait()
    own_store.wait()
    each(lambda e: out_copy(e).wait(), 1, nb)


def hand_over(attn_i, ssm_i, attn_o, ssm_o, sems):
    pieces = sems.shape[1] // 2
    size = attn_i.shape[0] // pieces
    copies = []
    for k, (src, dst) in enumerate([(attn_i, attn_o), (ssm_i, ssm_o)]):
        for p in range(pieces):
            at = pl.ds(p * size, size)
            copies.append(pltpu.make_async_copy(src.at[at], dst.at[at], sems.at[0, k * pieces + p]))
    for copy in copies:
        copy.start()
    for copy in copies:
        copy.wait()


def local(
    queries, kv_new, page_pool, page_owner, page_slot, prefix_len, suffix_len,
    ssm_in, b_in, c_in, step_size, decay_rate, skip_gain, prior_state,
):
    n = lax.axis_size("cache")
    nb = lax.axis_size("blk")
    tok = queries.shape[1]
    lists = page_owner.shape[2]
    lanes = nb * lists
    cap = max(16, max(2, 2 * lists // n) * nb)
    spots = page_pool.shape[1]
    spread_spots = max(spots, 128)
    vmem = pl.BlockSpec(memory_space=pltpu.VMEM)
    smem = pl.BlockSpec(memory_space=pltpu.SMEM)
    hbm = pl.BlockSpec(memory_space=pl.ANY)
    dma = pltpu.SemaphoreType.DMA
    wide = SH * HP
    rows = GROUP * tok
    most = max([nb * tok] + [PAGE * (high - low) for low, high, _ in phases_of(lanes, cap)])
    chunks = cap // CHUNK
    results = (
        jax.ShapeDtypeStruct((tok, QH * HD), BF16),
        jax.ShapeDtypeStruct((tok, wide), BF16),
    )
    attn, ssm = pl.pallas_call(
        functools.partial(kernel, n, nb, cap, lists, spots),
        out_shape=results,
        in_specs=[smem, smem, vmem, vmem, hbm, hbm, hbm, hbm, vmem, vmem, vmem, vmem, vmem, hbm],
        out_specs=(hbm, hbm),
        scratch_shapes=[
            pltpu.VMEM((8, lanes), jnp.int32),
            pltpu.VMEM((n, nb, 8, lanes), jnp.int32),
            pltpu.VMEM((2, spots * PAGE, HD), BF16),
            pltpu.VMEM((spots * PAGE, HD), F32),
            pltpu.VMEM((spots * PAGE, HD), F32),
            pltpu.VMEM((spread_spots, 2 * PAGE * HD), BF16),
            pltpu.VMEM((n, cap, 2 * PAGE * HD), BF16),
            pltpu.VMEM((n, cap, 2 * PAGE * HD), BF16),
            pltpu.VMEM((nb, tok, GROUP * HD), BF16),
            pltpu.VMEM((nb, tok, HD), BF16),
            pltpu.VMEM((nb, tok, HD), BF16),
            pltpu.VMEM((most, 2 * HD), BF16),
            pltpu.VMEM((most, HD), F32),
            pltpu.VMEM((HD, most), BF16),
            pltpu.VMEM((nb, 1, rows), F32),
            pltpu.VMEM((nb, 1, rows), F32),
            pltpu.VMEM((nb, HD, rows), F32),
            pltpu.VMEM((nb, tok, GROUP * HD), BF16),
            pltpu.VMEM((tok, wide), BF16),
            pltpu.VMEM((wide, NS), F32),
            pltpu.VMEM((tok, wide), F32),
            pltpu.VMEM((8, wide), F32),
            pltpu.VMEM((tok, wide), BF16),
            pltpu.VMEM((NS, wide), F32),
            pltpu.VMEM((tok, wide), BF16),
            pltpu.VMEM((NS, wide), BF16),
            pltpu.VMEM((NS, wide), BF16),
            dma((9,)), dma((n * nb,)), dma((n * nb,)), dma((n, chunks)), dma((n, chunks)),
            dma((nb,)), dma((nb,)), dma((nb,)), dma((nb,)), dma((nb,)), dma((nb,)),
            dma((nb,)), dma((nb,)), dma, dma,
        ],
        compiler_params=pltpu.CompilerParams(
            collective_id=0, has_side_effects=True, vmem_limit_bytes=56 * 1024 * 1024
        ),
    )(
        prefix_len, suffix_len, page_owner[0, 0, :, 0][None], page_slot[0], queries[0], kv_new[0],
        page_pool.reshape(spots * PAGE, 2 * KVH * HD), ssm_in[0], b_in[0], c_in[0], step_size[0].T,
        decay_rate[None, :], skip_gain[None, :], prior_state.reshape(wide, NS),
    )
    attn, ssm = pl.pallas_call(
        hand_over,
        out_shape=results,
        in_specs=[hbm, hbm],
        out_specs=(vmem, vmem),
        scratch_shapes=[dma((1, 4))],
    )(attn, ssm)
    return attn[None], ssm[None]


def solution(mesh):
    in_specs = (
        P(("groups", "cache"), "blk", None),
        P(("groups", "cache"), "blk", None),
        P(("groups", "cache"), None, None, None),
        P(("groups", "cache"), "blk", None, None),
        P(("groups", "cache"), "blk", None),
        P(("groups", "cache")),
        P(("groups", "cache")),
        P(("groups", "cache"), "blk", None),
        P(("groups", "cache"), "blk", None),
        P(("groups", "cache"), "blk", None),
        P(("groups", "cache"), "blk", None),
        P(),
        P(),
        P(("groups", "cache"), None, None, None),
    )
    out_specs = (P(("groups", "cache"), "blk", None), P(("groups", "cache"), "blk", None))
    return jax.shard_map(local, mesh=mesh, in_specs=in_specs, out_specs=out_specs, check_vma=False)
```

```python
import functools
import math

import jax
import jax.numpy as jnp
from jax import lax
from jax.experimental import pallas as pl
from jax.experimental.pallas import tpu as pltpu
from jax.sharding import PartitionSpec as P

QH = 16
KVH = 4
HD = 128
SH = 32
HP = 64
NS = 128
PAGE = 8
GROUP = QH // KVH
NEG = -1e30
CHUNK = 16
F32 = jnp.float32
BF16 = jnp.bfloat16


def remote(src, dst, send_sem, recv_sem, device):
    return pltpu.make_async_remote_copy(
        src_ref=src,
        dst_ref=dst,
        send_sem=send_sem,
        recv_sem=recv_sem,
        device_id=device,
        device_id_type=pl.DeviceIdType.MESH,
    )


def nt(a, b):
    return lax.dot_general(a, b, (((1,), (1,)), ((), ())), preferred_element_type=F32)


def nn(a, b):
    return jnp.dot(a, b, preferred_element_type=F32)


def iota(shape, axis):
    return lax.broadcasted_iota(jnp.int32, shape, axis)


def thirds(v):
    hi = v.astype(BF16).astype(F32)
    rest = v - hi
    mid = rest.astype(BF16).astype(F32)
    return [hi, mid, (rest - mid).astype(BF16).astype(F32)]


def phases_of(total, cap):
    found, done = [], 0
    for have in [cap - CHUNK, cap]:
        if have <= 0:
            continue
        late = total // cap * (cap - have) + max(total % cap - have, 0)
        ready = (total - late) // 16 * 16
        if ready > done:
            found.append((done, ready, have))
            done = ready
    return found


def kernel(
    n, nb, cap, lists, spots,
    plen, slen, owner, slot, q, kv, pool, x_hbm, b_rows, c_rows, dt_t, rate, skip, prior_hbm,
    attn_o, ssm_o,
    code, codes, praw, pf_k, pf_v, pmat, sendbuf, recv, qbuf, kbuf, vbuf, kx, vstage, vt, mbuf, lbuf, accbuf, obuf,
    x, prior, afull, skipf, xp, sbuf, hin, hout,
    loc, cs, cr, ps, pr, qs, qr, ks, kr, vs, vr, os, orr, hs, hr,
):
    me = lax.axis_index("cache")
    j = lax.axis_index("blk")
    tok = x.shape[0]
    wide = x.shape[1]
    width = GROUP * HD
    half = KVH * HD
    lanes = code.shape[1]
    rows = GROUP * tok
    prefix_limit = plen[0]
    suffix_limit = slen[0]
    chunks = cap // CHUNK

    def zpeer(d):
        return lax.rem(me + d, n)

    def bpeer(e):
        return lax.rem(j + e, nb)

    def cols(at, size):
        return pl.ds(pl.multiple_of(at, 128), size)

    loads = [
        pltpu.make_async_copy(x_hbm, x, loc.at[0]),
        pltpu.make_async_copy(pool.at[:, cols(j * HD, HD)], praw.at[0], loc.at[1]),
        pltpu.make_async_copy(pool.at[:, cols(half + j * HD, HD)], praw.at[1], loc.at[2]),
        pltpu.make_async_copy(q.at[:, cols(j * width, width)], qbuf.at[j], loc.at[3]),
        pltpu.make_async_copy(kv.at[:, cols(j * HD, HD)], kbuf.at[j], loc.at[4]),
        pltpu.make_async_copy(kv.at[:, cols(half + j * HD, HD)], vbuf.at[j], loc.at[5]),
    ]
    prior_load = pltpu.make_async_copy(prior_hbm, prior, loc.at[6])
    barrier = pltpu.get_barrier_semaphore()

    def greet(k, carry):
        peer = {"cache": zpeer(k // nb), "blk": bpeer(k % nb)}
        pl.semaphore_signal(barrier, inc=1, device_id=peer, device_id_type=pl.DeviceIdType.MESH)
        return carry

    if n * nb <= 16:
        for k in range(1, n * nb):
            greet(k, 0)
    else:
        lax.fori_loop(1, n * nb, greet, 0)
    for load in loads:
        load.start()

    @pl.when(j == 0)
    def _():
        prior_load.start()

    mine = iota((1, lanes), 1) // lists == j
    named_slots = slot[...] * n + owner[...]
    code[...] = jnp.where(mine, jnp.concatenate([named_slots] * nb, axis=1), 0)
    codes[me, j] = code[...]

    pl.semaphore_wait(barrier, n * nb - 1)

    def code_copy(k):
        peer = {"cache": zpeer(k // nb), "blk": bpeer(k % nb)}
        return remote(code, codes.at[me, j], cs.at[k], cr.at[k], peer)

    def q_copy(e):
        to = bpeer(e)
        return remote(q.at[:, cols(to * width, width)], qbuf.at[j], qs.at[e], qr.at[e], {"blk": to})

    def k_copy(e):
        to = bpeer(e)
        return remote(kv.at[:, cols(to * HD, HD)], kbuf.at[j], ks.at[e], kr.at[e], {"blk": to})

    def v_copy(e):
        to = bpeer(e)
        return remote(kv.at[:, cols(half + to * HD, HD)], vbuf.at[j], vs.at[e], vr.at[e], {"blk": to})

    def page_copy(d, c):
        at = pl.ds(c * CHUNK, CHUNK)
        return remote(sendbuf.at[d, at], recv.at[d, at], ps.at[d, c], pr.at[d, c], {"cache": zpeer(d)})

    def state_copy():
        return remote(hout, hin, hs, hr, {"blk": bpeer(1)})

    def out_copy(e):
        to = bpeer(e)
        return remote(obuf.at[to], attn_o.at[:, cols(j * width, width)], os.at[e], orr.at[e], {"blk": to})

    def each(what, low, high):
        if high - low <= 16:
            for i in range(low, high):
                what(i)
            return

        def body(i, carry):
            what(i)
            return carry

        lax.fori_loop(low, high, body, 0)

    def each_code(what):
        each(what, 1, n * nb)

    each_code(lambda k: code_copy(k).start())

    each(lambda e: (k_copy(e).start(), v_copy(e).start(), q_copy(e).start()), 1, nb)

    loads[1].wait()
    loads[2].wait()
    pf_k[...] = praw[0].astype(F32)
    pf_v[...] = praw[1].astype(F32)
    if spots < pmat.shape[0]:
        pmat[...] = jnp.zeros_like(pmat)
    for i in range(PAGE):
        at = pl.ds(i, spots, stride=PAGE)
        pmat[0:spots, i * HD : (i + 1) * HD] = pf_k[at, :].astype(BF16)
        pmat[0:spots, (PAGE + i) * HD : (PAGE + i + 1) * HD] = pf_v[at, :].astype(BF16)

    dt = dt_t[...].T
    fall = jnp.concatenate(thirds(dt * (-rate[...])), axis=0).astype(BF16)
    tri = jnp.where(iota((tok, 3 * tok), 0) >= lax.rem(iota((tok, 3 * tok), 1), tok), 1.0, 0.0).astype(BF16)
    logs = nn(tri, fall)
    gains = jnp.concatenate([jnp.exp(logs), jnp.broadcast_to(skip[...], (16, SH))], axis=0)
    a3 = jnp.concatenate(thirds(gains), axis=1).astype(BF16)
    b3 = jnp.concatenate(thirds(jnp.exp(-logs) * dt), axis=1).astype(BF16)
    lower = iota((tok, tok), 0) >= iota((tok, tok), 1)
    gram = jnp.where(lower, nt(c_rows[...], b_rows[...]), 0.0).astype(BF16)
    readout = jnp.concatenate([gram, c_rows[...]], axis=1)
    b_t = b_rows[...].astype(F32).T.astype(BF16)
    part = 2 * HD
    parts = wide // part

    loads[0].wait()

    def own_block(i, carry):
        at = cols(i * part, part)
        heads = lax.rem(iota((3 * SH, part), 0), SH)
        spread = jnp.where(heads == iota((3 * SH, part), 1) // HP + i * (part // HP), 1.0, 0.0).astype(BF16)
        grown = nn(a3, spread)
        afull[:, at] = grown[0:tok]
        skipf[:, at] = grown[tok : tok + 8]
        scaled = (nn(b3, spread) * x[:, at].astype(F32)).astype(BF16)
        xp[:, at] = scaled
        sbuf[:, at] = nn(b_t, scaled)
        return carry

    lax.fori_loop(0, parts, own_block, 0)

    def onward(i, carry):
        at = cols(i * part, part)
        hout[:, at] = (afull[tok - 1 : tok, at] * (hin[:, at].astype(F32) + sbuf[:, at])).astype(BF16)
        return carry

    before = jnp.where(iota((lanes, lanes), 0) < iota((lanes, lanes), 1), 1.0, 0.0).astype(BF16)

    def comb(r):
        both = jnp.sum(codes[r], axis=0)
        return lax.rem(both, n), both // n

    def ranked(named):
        flags = jnp.broadcast_to(jnp.where(named, 1.0, 0.0), (16, lanes)).astype(BF16)
        return nn(flags, before)[0:1].astype(jnp.int32)

    def onehot(flag):
        return jnp.where(flag, 1.0, 0.0).astype(BF16)

    each_code(lambda k: code_copy(k).wait_recv())
    spread_spots = pmat.shape[0]

    def answer(d):
        owners, slots = comb(zpeer(d))
        named = owners == me
        place = onehot((ranked(named) == iota((cap, lanes), 0)) & named)
        wants = onehot(slots == iota((spread_spots, lanes), 0))
        chosen = nt(place, wants).astype(BF16)
        for i in range(2 * PAGE * HD // part):
            sendbuf[d, :, i * part : (i + 1) * part] = nn(chosen, pmat[:, i * part : (i + 1) * part]).astype(BF16)
        page_copy(d, 0).start()

    each(answer, 1, n)
    for c in range(1, chunks):
        each(lambda d: page_copy(d, c).start(), 1, n)

    @pl.when(j == 0)
    def _():
        prior_load.wait()

        def fill(i, carry):
            at = cols(i * HD, HD)
            hin[:, at] = prior[at, :].T.astype(BF16)
            return carry

        lax.fori_loop(0, wide // HD, fill, 0)
        lax.fori_loop(0, parts, onward, 0)
        state_copy().start()

    owners, slots = comb(me)
    back = me - owners
    away = jnp.where(back < 0, back + n, back)
    rank = jnp.zeros((1, lanes), jnp.int32)

    def add_rank(d, rank):
        named = away == d
        return rank + jnp.where(named, ranked(named), 0)

    if n <= 8:
        for d in range(1, n):
            rank = add_rank(d, rank)
    else:
        rank = lax.fori_loop(1, n, add_rank, rank)
    lane = iota((1, lanes), 1)
    turn = jnp.where(away == 0, 0, rank // CHUNK) * lanes + lane
    turn_f = turn.astype(F32)
    turn_col = jnp.broadcast_to(turn_f, (lanes, lanes)).T
    ahead = jnp.where(turn_col < turn_f, 1.0, 0.0)
    spot = jnp.sum(ahead, axis=0, keepdims=True).astype(jnp.int32)
    sorted_f = jnp.where(iota((lanes, lanes), 0) == spot, 1.0, 0.0)
    sorting = sorted_f.astype(BF16)
    number = (lax.rem(lane, lists) * nb + lane // lists).astype(F32)
    first_row = jnp.sum(sorted_f * number, axis=1, keepdims=True).astype(jnp.int32) * PAGE
    own_wants = onehot((slots == iota((spread_spots, lanes), 0)) & (away == 0))
    places = [onehot((rank == iota((cap, lanes), 0)) & (away == d)) for d in range(1, n)]

    def read_block():
        alive = j * tok + iota((tok, part), 0) < suffix_limit

        def body(i, carry):
            at = cols(i * part, part)
            both = jnp.concatenate([xp[:, at], hin[:, at]], axis=0)
            total = afull[:, at] * nn(readout, both) + skipf[0:1, at] * x[:, at].astype(F32)
            ssm_o[:, at] = jnp.where(alive, total, 0.0).astype(BF16)
            return carry

        lax.fori_loop(0, parts, body, 0)

    def chain():
        state_copy().wait_recv()

        @pl.when(j < nb - 1)
        def _():
            lax.fori_loop(0, parts, onward, 0)
            state_copy().start()

        read_block()

    pl.when(j == 0)(read_block)
    pl.when(j == 1)(chain)

    rate2 = math.log2(math.e) / math.sqrt(HD)
    first_lane = iota((1, HD), 1) == 0
    one_column = jnp.broadcast_to(jnp.where(first_lane, 1.0, 0.0), (tok, HD)).astype(BF16)

    def queries(b):
        pieces = [jnp.concatenate([qbuf[b, :, h * HD : (h + 1) * HD], one_column], axis=1) for h in range(GROUP)]
        return jnp.concatenate(pieces, axis=0)

    def bias(visible, size):
        column = jnp.where(visible, 0.0, NEG)
        return jnp.where(first_lane, jnp.broadcast_to(column, (size, HD)), 0.0).astype(BF16)

    for load in loads[3:]:
        load.wait()
    each(lambda e: (k_copy(e).wait_recv(), v_copy(e).wait_recv(), q_copy(e).wait_recv()), 1, nb)

    for b in range(nb):
        kx[b * tok : (b + 1) * tok, 0:HD] = kbuf[b]
        kx[b * tok : (b + 1) * tok, HD : 2 * HD] = bias(b * tok + iota((tok, 1), 0) < suffix_limit, tok)
        vt[:, b * tok : (b + 1) * tok] = vbuf[b].astype(F32).T.astype(BF16)
    causal = jnp.where(iota((tok, rows), 0) <= lax.rem(iota((tok, rows), 1), tok), 0.0, NEG)
    for b in range(nb):
        count = (b + 1) * tok
        qb = queries(b)
        scores = nt(kx[0:count, :], qb)
        near = scores[count - tok :] + causal
        scores = near if b == 0 else jnp.concatenate([scores[: count - tok], near], axis=0)
        top = jnp.max(scores, axis=0, keepdims=True) * rate2
        weights = jnp.exp2(scores * rate2 - top)
        mbuf[b] = top
        lbuf[b] = jnp.sum(weights, axis=0, keepdims=True)
        accbuf[b] = nn(vt[:, 0:count], weights.astype(BF16))

    pl.when(j >= 2)(chain)

    phases = phases_of(lanes, cap)
    arrived = 0
    picks = []
    for low, high, have in phases:
        table = jnp.concatenate([own_wants] + [p[0:have] for p in places], axis=0)
        picks.append(nt(sorting[low:high], table).astype(BF16))
    if nb == 4:
        over = 1 + 2 * lax.rem(j + 1, 2)
        order = [2, over, nb - over, nb]
    else:
        order = list(range(1, nb + 1))
    for pick, (low, high, have) in zip(picks, phases):
        last = high == lanes
        for c in range(arrived, have // CHUNK):
            each(lambda d: page_copy(d, c).wait_recv(), 1, n)
        arrived = have // CHUNK
        pages = high - low
        for i in range(2 * PAGE * HD // part):
            at = slice(i * part, (i + 1) * part)
            got = recv[1:n, 0:have, at].reshape((n - 1) * have, part)
            out = nn(pick, jnp.concatenate([pmat[:, at], got], axis=0))
            for k in range(2):
                row = 2 * i + k
                piece = out[:, k * HD : (k + 1) * HD]
                if row < PAGE:
                    kx[row * pages : (row + 1) * pages, 0:HD] = piece.astype(BF16)
                    kx[row * pages : (row + 1) * pages, HD : 2 * HD] = bias(first_row[low:high] + row < prefix_limit, pages)
                else:
                    vstage[(row - PAGE) * pages : (row - PAGE + 1) * pages, :] = piece
        count = PAGE * pages
        for i in range(count // HD):
            vt[:, i * HD : (i + 1) * HD] = vstage[i * HD : (i + 1) * HD, :].T.astype(BF16)

        for turn, e in enumerate(order):
            b = bpeer(e)
            scores = nt(kx[0:count, :], queries(b))
            old = mbuf[b]
            top = jnp.maximum(jnp.max(scores, axis=0, keepdims=True) * rate2, old)
            weights = jnp.exp2(scores * rate2 - top)
            factor = jnp.exp2(old - top)
            total = jnp.sum(weights, axis=0, keepdims=True) + lbuf[b] * factor
            mixed = nn(vt[:, 0:count], weights.astype(BF16)) + accbuf[b] * factor
            if not last:
                mbuf[b] = top
                lbuf[b] = total
                accbuf[b] = mixed
            else:
                alive = b * tok + lax.rem(iota((1, rows), 1), tok) < suffix_limit
                final = mixed * jnp.where(alive, 1.0 / total, 0.0)
                heads = [final[:, h * tok : (h + 1) * tok].T.astype(BF16) for h in range(GROUP)]
                result = jnp.concatenate(heads, axis=1)
                if turn < nb - 1:
                    obuf[b] = result
                    out_copy(e).start()
                else:
                    attn_o[:, cols(j * width, width)] = result

    each_code(lambda k: code_copy(k).wait_send())
    each(lambda e: (q_copy(e).wait_send(), k_copy(e).wait_send(), v_copy(e).wait_send()), 1, nb)
    for c in range(chunks):
        each(lambda d: page_copy(d, c).wait_send(), 1, n)

    @pl.when(j < nb - 1)
    def _():
        state_copy().wait_send()

    each(lambda e: out_copy(e).wait(), 1, nb)


def local(
    queries, kv_new, page_pool, page_owner, page_slot, prefix_len, suffix_len,
    ssm_in, b_in, c_in, step_size, decay_rate, skip_gain, prior_state,
):
    n = lax.axis_size("cache")
    nb = lax.axis_size("blk")
    tok = queries.shape[1]
    lists = page_owner.shape[2]
    lanes = nb * lists
    cap = max(16, max(2, 2 * lists // n) * nb)
    spots = page_pool.shape[1]
    spread_spots = max(spots, 128)
    vmem = pl.BlockSpec(memory_space=pltpu.VMEM)
    smem = pl.BlockSpec(memory_space=pltpu.SMEM)
    hbm = pl.BlockSpec(memory_space=pltpu.HBM)
    dma = pltpu.SemaphoreType.DMA
    wide = SH * HP
    rows = GROUP * tok
    most = max([nb * tok] + [PAGE * (high - low) for low, high, _ in phases_of(lanes, cap)])
    chunks = cap // CHUNK
    results = (
        jax.ShapeDtypeStruct((tok, QH * HD), BF16),
        jax.ShapeDtypeStruct((tok, wide), BF16),
    )
    attn, ssm = pl.pallas_call(
        functools.partial(kernel, n, nb, cap, lists, spots),
        out_shape=tuple(pltpu.VMEM(r.shape, r.dtype) for r in results),
        in_specs=[smem, smem, vmem, vmem, hbm, hbm, hbm, hbm, vmem, vmem, vmem, vmem, vmem, hbm],
        out_specs=(vmem, vmem),
        scratch_shapes=[
            pltpu.VMEM((1, lanes), jnp.int32),
            pltpu.VMEM((n, nb, 1, lanes), jnp.int32),
            pltpu.VMEM((2, spots * PAGE, HD), BF16),
            pltpu.VMEM((spots * PAGE, HD), F32),
            pltpu.VMEM((spots * PAGE, HD), F32),
            pltpu.VMEM((spread_spots, 2 * PAGE * HD), BF16),
            pltpu.VMEM((n, cap, 2 * PAGE * HD), BF16),
            pltpu.VMEM((n, cap, 2 * PAGE * HD), BF16),
            pltpu.VMEM((nb, tok, GROUP * HD), BF16),
            pltpu.VMEM((nb, tok, HD), BF16),
            pltpu.VMEM((nb, tok, HD), BF16),
            pltpu.VMEM((most, 2 * HD), BF16),
            pltpu.VMEM((most, HD), F32),
            pltpu.VMEM((HD, most), BF16),
            pltpu.VMEM((nb, 1, rows), F32),
            pltpu.VMEM((nb, 1, rows), F32),
            pltpu.VMEM((nb, HD, rows), F32),
            pltpu.VMEM((nb, tok, GROUP * HD), BF16),
            pltpu.VMEM((tok, wide), BF16),
            pltpu.VMEM((wide, NS), F32),
            pltpu.VMEM((tok, wide), F32),
            pltpu.VMEM((8, wide), F32),
            pltpu.VMEM((tok, wide), BF16),
            pltpu.VMEM((NS, wide), F32),
            pltpu.VMEM((NS, wide), BF16),
            pltpu.VMEM((NS, wide), BF16),
            dma((7,)), dma((n * nb,)), dma((n * nb,)), dma((n, chunks)), dma((n, chunks)),
            dma((nb,)), dma((nb,)), dma((nb,)), dma((nb,)), dma((nb,)), dma((nb,)),
            dma((nb,)), dma((nb,)), dma, dma,
        ],
        compiler_params=pltpu.CompilerParams(
            collective_id=0, has_side_effects=True, vmem_limit_bytes=56 * 1024 * 1024
        ),
    )(
        prefix_len, suffix_len, page_owner[0, 0, :, 0][None], page_slot[0], queries[0], kv_new[0],
        page_pool.reshape(spots * PAGE, 2 * KVH * HD), ssm_in[0], b_in[0], c_in[0], step_size[0].T,
        decay_rate[None, :], skip_gain[None, :], prior_state.reshape(wide, NS),
    )
    return attn[None], ssm[None]


def solution(mesh):
    in_specs = (
        P(("groups", "cache"), "blk", None),
        P(("groups", "cache"), "blk", None),
        P(("groups", "cache"), None, None, None),
        P(("groups", "cache"), "blk", None, None),
        P(("groups", "cache"), "blk", None),
        P(("groups", "cache")),
        P(("groups", "cache")),
        P(("groups", "cache"), "blk", None),
        P(("groups", "cache"), "blk", None),
        P(("groups", "cache"), "blk", None),
        P(("groups", "cache"), "blk", None),
        P(),
        P(),
        P(("groups", "cache"), None, None, None),
    )
    out_specs = (P(("groups", "cache"), "blk", None), P(("groups", "cache"), "blk", None))
    return jax.shard_map(local, mesh=mesh, in_specs=in_specs, out_specs=out_specs, check_vma=False)
```

```python
import functools
import math

import jax
import jax.numpy as jnp
from jax import lax
from jax.experimental import pallas as pl
from jax.experimental.pallas import tpu as pltpu
from jax.sharding import PartitionSpec as P

QH = 16
KVH = 4
HD = 128
SH = 32
HP = 64
NS = 128
PAGE = 8
GROUP = QH // KVH
NEG = -1e30
PIECES = 2
PD = HD // PIECES
F32 = jnp.float32
BF16 = jnp.bfloat16


def remote(src, dst, send_sem, recv_sem, device):
    return pltpu.make_async_remote_copy(
        src_ref=src,
        dst_ref=dst,
        send_sem=send_sem,
        recv_sem=recv_sem,
        device_id=device,
        device_id_type=pl.DeviceIdType.MESH,
    )


def nt(a, b):
    return lax.dot_general(a, b, (((1,), (1,)), ((), ())), preferred_element_type=F32)


def nn(a, b):
    return jnp.dot(a, b, preferred_element_type=F32)


def iota(shape, axis):
    return lax.broadcasted_iota(jnp.int32, shape, axis)


def thirds(v):
    hi = v.astype(BF16).astype(F32)
    rest = v - hi
    mid = rest.astype(BF16).astype(F32)
    return [hi, mid, (rest - mid).astype(BF16).astype(F32)]


def kernel(
    n, nb, cap, lists, spots,
    plen, slen, owner, slot, q, kv, pool, x_hbm, b_rows, c_rows, dt_t, rate, skip, prior_hbm,
    attn_o, ssm_o,
    code, codes, praw, pf_k, pf_v, pmat, sendbuf, recv, qbuf, kbuf, vbuf, kx, vt, vpart, mbuf, lbuf, accbuf, wbuf, obuf, ostage,
    x, prior, afull, skipf, xp, sbuf, hin, hout,
    loc, cs, cr, ps, pr, qs, qr, ks, kr, vs, vr, os, orr, hs, hr,
):
    me = lax.axis_index("cache")
    j = lax.axis_index("blk")
    tok = x.shape[0]
    wide = x.shape[1]
    width = GROUP * HD
    half = KVH * HD
    lanes = code.shape[1]
    rows = GROUP * tok
    prefix_limit = plen[0]
    suffix_limit = slen[0]
    part = 2 * HD
    parts = wide // part

    def zpeer(d):
        return lax.rem(me + d, n)

    def bpeer(e):
        return lax.rem(j + e, nb)

    def cols(at, size):
        return pl.ds(pl.multiple_of(at, 128), size)

    loads = [
        pltpu.make_async_copy(pool.at[:, cols(j * HD, HD)], praw.at[0], loc.at[0]),
        pltpu.make_async_copy(pool.at[:, cols(half + j * HD, HD)], praw.at[1], loc.at[1]),
        pltpu.make_async_copy(x_hbm, x, loc.at[2]),
        pltpu.make_async_copy(q.at[:, cols(j * width, width)], qbuf.at[j], loc.at[3]),
        pltpu.make_async_copy(kv.at[:, cols(j * HD, HD)], kbuf.at[j], loc.at[4]),
        pltpu.make_async_copy(kv.at[:, cols(half + j * HD, HD)], vbuf.at[j], loc.at[5]),
    ]
    prior_load = pltpu.make_async_copy(prior_hbm, prior, loc.at[6])
    barrier = pltpu.get_barrier_semaphore()

    def greet(k, carry):
        peer = {"cache": zpeer(k // nb), "blk": bpeer(k % nb)}
        pl.semaphore_signal(barrier, inc=1, device_id=peer, device_id_type=pl.DeviceIdType.MESH)
        return carry

    if n * nb <= 16:
        for k in range(1, n * nb):
            greet(k, 0)
    else:
        lax.fori_loop(1, n * nb, greet, 0)
    mine = iota((1, lanes), 1) // lists == j
    named_slots = slot[...] * n + owner[...]
    code[...] = jnp.where(mine, jnp.concatenate([named_slots] * nb, axis=1), 0)
    codes[me, j] = code[...]

    pl.semaphore_wait(barrier, n * nb - 1)

    def code_copy(k):
        peer = {"cache": zpeer(k // nb), "blk": bpeer(k % nb)}
        return remote(code, codes.at[me, j], cs.at[k], cr.at[k], peer)

    def q_copy(e):
        to = bpeer(e)
        return remote(q.at[:, cols(to * width, width)], qbuf.at[j], qs.at[e], qr.at[e], {"blk": to})

    def k_copy(e):
        to = bpeer(e)
        return remote(kv.at[:, cols(to * HD, HD)], kbuf.at[j], ks.at[e], kr.at[e], {"blk": to})

    def v_copy(e):
        to = bpeer(e)
        return remote(kv.at[:, cols(half + to * HD, HD)], vbuf.at[j], vs.at[e], vr.at[e], {"blk": to})

    def page_copy(d, c):
        at = pl.ds(0, PAGE * HD) if c == 0 else pl.ds(PAGE * HD + (c - 1) * PAGE * PD, PAGE * PD)
        return remote(sendbuf.at[d, :, at], recv.at[d, :, at], ps.at[d, c], pr.at[d, c], {"cache": zpeer(d)})

    def state_copy():
        return remote(hout, hin, hs, hr, {"blk": bpeer(1)})

    def out_copy(e, s):
        to = bpeer(e)
        return remote(obuf.at[s, to], ostage.at[s, j], os.at[e, s], orr.at[e, s], {"blk": to})

    def each(what, low, high):
        if high - low <= 16:
            for i in range(low, high):
                what(i)
            return

        def body(i, carry):
            what(i)
            return carry

        lax.fori_loop(low, high, body, 0)

    def each_code(what):
        each(what, 1, n * nb)

    each_code(lambda k: code_copy(k).start())
    for load in loads:
        load.start()

    @pl.when(j == 0)
    def _():
        prior_load.start()

    loads[0].wait()
    loads[1].wait()
    pf_k[...] = praw[0].astype(F32)
    pf_v[...] = praw[1].astype(F32)
    if spots < pmat.shape[0]:
        pmat[...] = jnp.zeros_like(pmat)
    values = []
    for i in range(PAGE):
        at = pl.ds(i, spots, stride=PAGE)
        pmat[0:spots, i * HD : (i + 1) * HD] = pf_k[at, :].astype(BF16)
        values.append(pf_v[at, :])
    for s in range(PIECES):
        for t in range(PAGE // PIECES):
            tile = [values[t * PIECES + k][:, s * PD : (s + 1) * PD] for k in range(PIECES)]
            at = PAGE * HD + s * PAGE * PD + t * HD
            pmat[0:spots, at : at + HD] = jnp.concatenate(tile, axis=1).astype(BF16)

    @pl.when(j == 0)
    def _():
        prior_load.wait()

        def fill(i, carry):
            at = cols(i * HD, HD)
            hin[:, at] = prior[at, :].T.astype(BF16)
            return carry

        lax.fori_loop(0, wide // HD, fill, 0)

    before = jnp.where(iota((lanes, lanes), 0) < iota((lanes, lanes), 1), 1.0, 0.0).astype(BF16)

    def comb(r):
        both = jnp.sum(codes[r], axis=0)
        return lax.rem(both, n), both // n

    def ranked(named):
        flags = jnp.broadcast_to(jnp.where(named, 1.0, 0.0), (16, lanes)).astype(BF16)
        return nn(flags, before)[0:1].astype(jnp.int32)

    def onehot(flag):
        return jnp.where(flag, 1.0, 0.0).astype(BF16)

    each_code(lambda k: code_copy(k).wait_recv())
    spread_spots = pmat.shape[0]

    def chosen_for(d):
        owners, slots = comb(zpeer(d))
        named = owners == me
        place = onehot((ranked(named) == iota((cap, lanes), 0)) & named)
        wants = onehot(slots == iota((spread_spots, lanes), 0))
        return nt(place, wants).astype(BF16)

    def answer(d, chosen, c):
        low = 0 if c == 0 else PAGE * HD + (c - 1) * PAGE * PD
        high = PAGE * HD + c * PAGE * PD
        for at in range(low, high, part):
            sendbuf[d, :, at : at + part] = nn(chosen, pmat[:, at : at + part]).astype(BF16)
        page_copy(d, c).start()

    if n <= 8:
        wanted = [chosen_for(d) for d in range(1, n)]
        for c in range(1 + PIECES):
            for d in range(1, n):
                answer(d, wanted[d - 1], c)
    else:
        def answer_all(d):
            chosen = chosen_for(d)
            for c in range(1 + PIECES):
                answer(d, chosen, c)

        each(answer_all, 1, n)
    each(lambda e: (k_copy(e).start(), v_copy(e).start(), q_copy(e).start()), 1, nb)

    dt = dt_t[...].T
    fall = jnp.concatenate(thirds(dt * (-rate[...])), axis=0).astype(BF16)
    tri = jnp.where(iota((tok, 3 * tok), 0) >= lax.rem(iota((tok, 3 * tok), 1), tok), 1.0, 0.0).astype(BF16)
    logs = nn(tri, fall)
    gains = jnp.concatenate([jnp.exp(logs), jnp.broadcast_to(skip[...], (16, SH))], axis=0)
    a3 = jnp.concatenate(thirds(gains), axis=1).astype(BF16)
    b3 = jnp.concatenate(thirds(jnp.exp(-logs) * dt), axis=1).astype(BF16)
    lower = iota((tok, tok), 0) >= iota((tok, tok), 1)
    gram = jnp.where(lower, nt(c_rows[...], b_rows[...]), 0.0).astype(BF16)
    readout = jnp.concatenate([gram, c_rows[...]], axis=1)
    b_t = b_rows[...].astype(F32).T.astype(BF16)

    loads[2].wait()

    def own_block(i, carry):
        at = cols(i * part, part)
        heads = lax.rem(iota((3 * SH, part), 0), SH)
        spread = jnp.where(heads == iota((3 * SH, part), 1) // HP + i * (part // HP), 1.0, 0.0).astype(BF16)
        grown = nn(a3, spread)
        afull[:, at] = grown[0:tok]
        skipf[:, at] = grown[tok : tok + 8]
        scaled = (nn(b3, spread) * x[:, at].astype(F32)).astype(BF16)
        xp[:, at] = scaled
        sbuf[:, at] = nn(b_t, scaled)
        return carry

    lax.fori_loop(0, parts, own_block, 0)

    def onward(i, carry):
        at = cols(i * part, part)
        hout[:, at] = (afull[tok - 1 : tok, at] * (hin[:, at].astype(F32) + sbuf[:, at])).astype(BF16)
        return carry

    @pl.when(j == 0)
    def _():
        lax.fori_loop(0, parts, onward, 0)
        state_copy().start()

    owners, slots = comb(me)
    back = me - owners
    away = jnp.where(back < 0, back + n, back)
    rank = jnp.zeros((1, lanes), jnp.int32)

    def add_rank(d, rank):
        named = away == d
        return rank + jnp.where(named, ranked(named), 0)

    if n <= 8:
        for d in range(1, n):
            rank = add_rank(d, rank)
    else:
        rank = lax.fori_loop(1, n, add_rank, rank)
    page = iota((lanes, 1), 0)
    first_row = (lax.rem(page, lists) * nb + page // lists) * PAGE
    same = jnp.where(iota((lanes, lanes), 0) == iota((lanes, lanes), 1), 1.0, 0.0).astype(BF16)
    own_wants = onehot((slots == iota((spread_spots, lanes), 0)) & (away == 0))
    places = [onehot((rank == iota((cap, lanes), 0)) & (away == d)) for d in range(1, n)]

    def read_block():
        alive = j * tok + iota((tok, part), 0) < suffix_limit

        def body(i, carry):
            at = cols(i * part, part)
            both = jnp.concatenate([xp[:, at], hin[:, at]], axis=0)
            total = afull[:, at] * nn(readout, both) + skipf[0:1, at] * x[:, at].astype(F32)
            ssm_o[:, at] = jnp.where(alive, total, 0.0).astype(BF16)
            return carry

        lax.fori_loop(0, parts, body, 0)

    def chain():
        state_copy().wait_recv()

        @pl.when(j < nb - 1)
        def _():
            lax.fori_loop(0, parts, onward, 0)
            state_copy().start()

        read_block()

    pl.when(j == 0)(read_block)
    pl.when(j == 1)(chain)

    rate2 = math.log2(math.e) / math.sqrt(HD)
    first_lane = iota((1, HD), 1) == 0
    one_column = jnp.broadcast_to(jnp.where(first_lane, 1.0, 0.0), (tok, HD)).astype(BF16)

    def queries(b):
        pieces = [jnp.concatenate([qbuf[b, :, h * HD : (h + 1) * HD], one_column], axis=1) for h in range(GROUP)]
        return jnp.concatenate(pieces, axis=0)

    def bias(visible, size):
        column = jnp.where(visible, 0.0, NEG)
        return jnp.where(first_lane, jnp.broadcast_to(column, (size, HD)), 0.0).astype(BF16)

    for load in loads[3:]:
        load.wait()
    each(lambda e: (k_copy(e).wait_recv(), v_copy(e).wait_recv(), q_copy(e).wait_recv()), 1, nb)

    for b in range(nb):
        kx[b * tok : (b + 1) * tok, 0:HD] = kbuf[b]
        kx[b * tok : (b + 1) * tok, HD : 2 * HD] = bias(b * tok + iota((tok, 1), 0) < suffix_limit, tok)
        vt[:, b * tok : (b + 1) * tok] = vbuf[b].astype(F32).T.astype(BF16)
    causal = jnp.where(iota((tok, rows), 0) <= lax.rem(iota((tok, rows), 1), tok), 0.0, NEG)
    for b in range(nb):
        count = (b + 1) * tok
        qb = queries(b)
        scores = nt(kx[0:count, :], qb)
        near = scores[count - tok :] + causal
        scores = near if b == 0 else jnp.concatenate([scores[: count - tok], near], axis=0)
        top = jnp.max(scores, axis=0, keepdims=True) * rate2
        weights = jnp.exp2(scores * rate2 - top)
        mbuf[b] = top
        lbuf[b] = jnp.sum(weights, axis=0, keepdims=True)
        accbuf[b] = nn(vt[:, 0:count], weights.astype(BF16))

    table = jnp.concatenate([own_wants] + places, axis=0)
    pick = nt(same, table).astype(BF16)
    if nb == 4:
        over = 1 + 2 * lax.rem(j + 1, 2)
        order = [2, over, nb - over, nb]
    else:
        order = list(range(1, nb + 1))

    def gathered(at):
        got = recv[1:n, :, at : at + part].reshape((n - 1) * cap, part)
        return nn(pick, jnp.concatenate([pmat[:, at : at + part], got], axis=0))

    count = PAGE * lanes
    for i in range(PAGE):
        kx[i * lanes : (i + 1) * lanes, HD : 2 * HD] = bias(first_row + i < prefix_limit, lanes)
    each(lambda d: page_copy(d, 0).wait_recv(), 1, n)
    for at in range(0, PAGE * HD, part):
        out = gathered(at).astype(BF16)
        i = at // HD
        kx[i * lanes : (i + 1) * lanes, 0:HD] = out[:, 0:HD]
        kx[(i + 1) * lanes : (i + 2) * lanes, 0:HD] = out[:, HD : 2 * HD]
    for b in range(nb):
        scores = nt(kx[0:count, :], queries(b))
        old = mbuf[b]
        top = jnp.maximum(jnp.max(scores, axis=0, keepdims=True) * rate2, old)
        weights = jnp.exp2(scores * rate2 - top)
        factor = jnp.exp2(old - top)
        total = jnp.sum(weights, axis=0, keepdims=True) + lbuf[b] * factor
        alive = b * tok + lax.rem(iota((1, rows), 1), tok) < suffix_limit
        lbuf[b] = jnp.where(alive, 1.0 / total, 0.0)
        accbuf[b] = accbuf[b] * factor
        wbuf[b] = weights.astype(BF16)

    pl.when(j == 2)(chain)

    for s in range(PIECES):
        if s == PIECES - 1:
            pl.when(j > 2)(chain)
        each(lambda d: page_copy(d, 1 + s).wait_recv(), 1, n)
        for i in range(PAGE * PD // part):
            out = gathered(PAGE * HD + s * PAGE * PD + i * part)
            for t in range(2):
                turned = out[:, t * HD : (t + 1) * HD].T.astype(BF16)
                for k in range(PIECES):
                    row = (2 * i + t) * PIECES + k
                    vpart[:, row * lanes : (row + 1) * lanes] = turned[k * PD : (k + 1) * PD]
        for turn, e in enumerate(order):
            b = bpeer(e)
            final = (nn(vpart[...], wbuf[b]) + accbuf[b, s * PD : (s + 1) * PD]) * lbuf[b]
            heads = jnp.concatenate([final[:, h * tok : (h + 1) * tok] for h in range(GROUP)], axis=0)
            result = heads.T.astype(BF16)
            if turn < nb - 1:
                obuf[s, b] = result
                out_copy(e, s).start()
            else:
                ostage[s, j] = result

    each_code(lambda k: code_copy(k).wait_send())
    each(lambda e: (q_copy(e).wait_send(), k_copy(e).wait_send(), v_copy(e).wait_send()), 1, nb)
    for c in range(1 + PIECES):
        each(lambda d: page_copy(d, c).wait_send(), 1, n)

    @pl.when(j < nb - 1)
    def _():
        state_copy().wait_send()

    for s in range(PIECES):
        each(lambda e: out_copy(e, s).wait(), 1, nb)
    for b in range(nb):
        for h in range(GROUP):
            pieces = [ostage[s, b, :, h * PD : (h + 1) * PD] for s in range(PIECES)]
            attn_o[:, b * width + h * HD : b * width + (h + 1) * HD] = jnp.concatenate(pieces, axis=1)


def local(
    queries, kv_new, page_pool, page_owner, page_slot, prefix_len, suffix_len,
    ssm_in, b_in, c_in, step_size, decay_rate, skip_gain, prior_state,
):
    n = lax.axis_size("cache")
    nb = lax.axis_size("blk")
    tok = queries.shape[1]
    lists = page_owner.shape[2]
    lanes = nb * lists
    cap = max(16, max(2, 2 * lists // n) * nb)
    spots = page_pool.shape[1]
    spread_spots = max(spots, 128)
    vmem = pl.BlockSpec(memory_space=pltpu.VMEM)
    smem = pl.BlockSpec(memory_space=pltpu.SMEM)
    hbm = pl.BlockSpec(memory_space=pltpu.HBM)
    dma = pltpu.SemaphoreType.DMA
    wide = SH * HP
    rows = GROUP * tok
    most = max(nb * tok, PAGE * lanes)
    results = (
        jax.ShapeDtypeStruct((tok, QH * HD), BF16),
        jax.ShapeDtypeStruct((tok, wide), BF16),
    )
    attn, ssm = pl.pallas_call(
        functools.partial(kernel, n, nb, cap, lists, spots),
        out_shape=tuple(pltpu.VMEM(r.shape, r.dtype) for r in results),
        in_specs=[smem, smem, vmem, vmem, hbm, hbm, hbm, hbm, vmem, vmem, vmem, vmem, vmem, hbm],
        out_specs=(vmem, vmem),
        scratch_shapes=[
            pltpu.VMEM((1, lanes), jnp.int32),
            pltpu.VMEM((n, nb, 1, lanes), jnp.int32),
            pltpu.VMEM((2, spots * PAGE, HD), BF16),
            pltpu.VMEM((spots * PAGE, HD), F32),
            pltpu.VMEM((spots * PAGE, HD), F32),
            pltpu.VMEM((spread_spots, 2 * PAGE * HD), BF16),
            pltpu.VMEM((n, cap, 2 * PAGE * HD), BF16),
            pltpu.VMEM((n, cap, 2 * PAGE * HD), BF16),
            pltpu.VMEM((nb, tok, GROUP * HD), BF16),
            pltpu.VMEM((nb, tok, HD), BF16),
            pltpu.VMEM((nb, tok, HD), BF16),
            pltpu.VMEM((most, 2 * HD), BF16),
            pltpu.VMEM((HD, nb * tok), BF16),
            pltpu.VMEM((PD, PAGE * lanes), BF16),
            pltpu.VMEM((nb, 1, rows), F32),
            pltpu.VMEM((nb, 1, rows), F32),
            pltpu.VMEM((nb, HD, rows), F32),
            pltpu.VMEM((nb, PAGE * lanes, rows), BF16),
            pltpu.VMEM((PIECES, nb, tok, GROUP * PD), BF16),
            pltpu.VMEM((PIECES, nb, tok, GROUP * PD), BF16),
            pltpu.VMEM((tok, wide), BF16),
            pltpu.VMEM((wide, NS), F32),
            pltpu.VMEM((tok, wide), F32),
            pltpu.VMEM((8, wide), F32),
            pltpu.VMEM((tok, wide), BF16),
            pltpu.VMEM((NS, wide), F32),
            pltpu.VMEM((NS, wide), BF16),
            pltpu.VMEM((NS, wide), BF16),
            dma((7,)), dma((n * nb,)), dma((n * nb,)), dma((n, 1 + PIECES)), dma((n, 1 + PIECES)),
            dma((nb,)), dma((nb,)), dma((nb,)), dma((nb,)), dma((nb,)), dma((nb,)),
            dma((nb, PIECES)), dma((nb, PIECES)), dma, dma,
        ],
        compiler_params=pltpu.CompilerParams(
            collective_id=0, has_side_effects=True, vmem_limit_bytes=56 * 1024 * 1024
        ),
    )(
        prefix_len, suffix_len, page_owner[0, 0, :, 0][None], page_slot[0], queries[0], kv_new[0],
        page_pool.reshape(spots * PAGE, 2 * KVH * HD), ssm_in[0], b_in[0], c_in[0], step_size[0].T,
        decay_rate[None, :], skip_gain[None, :], prior_state.reshape(wide, NS),
    )
    return attn[None], ssm[None]


def solution(mesh):
    in_specs = (
        P(("groups", "cache"), "blk", None),
        P(("groups", "cache"), "blk", None),
        P(("groups", "cache"), None, None, None),
        P(("groups", "cache"), "blk", None, None),
        P(("groups", "cache"), "blk", None),
        P(("groups", "cache")),
        P(("groups", "cache")),
        P(("groups", "cache"), "blk", None),
        P(("groups", "cache"), "blk", None),
        P(("groups", "cache"), "blk", None),
        P(("groups", "cache"), "blk", None),
        P(),
        P(),
        P(("groups", "cache"), None, None, None),
    )
    out_specs = (P(("groups", "cache"), "blk", None), P(("groups", "cache"), "blk", None))
    return jax.shard_map(local, mesh=mesh, in_specs=in_specs, out_specs=out_specs, check_vma=False)
```

```python
import functools
import math

import jax
import jax.numpy as jnp
from jax import lax
from jax.experimental import pallas as pl
from jax.experimental.pallas import tpu as pltpu
from jax.sharding import PartitionSpec as P

QH = 16
KVH = 4
HD = 128
SH = 32
HP = 64
NS = 128
PAGE = 8
GROUP = QH // KVH
NEG = -1e30
PIECES = 2
PD = HD // PIECES
F32 = jnp.float32
BF16 = jnp.bfloat16


def remote(src, dst, send_sem, recv_sem, device):
    return pltpu.make_async_remote_copy(
        src_ref=src,
        dst_ref=dst,
        send_sem=send_sem,
        recv_sem=recv_sem,
        device_id=device,
        device_id_type=pl.DeviceIdType.MESH,
    )


def nt(a, b):
    return lax.dot_general(a, b, (((1,), (1,)), ((), ())), preferred_element_type=F32)


def nn(a, b):
    return jnp.dot(a, b, preferred_element_type=F32)


def iota(shape, axis):
    return lax.broadcasted_iota(jnp.int32, shape, axis)


def thirds(v):
    hi = v.astype(BF16).astype(F32)
    rest = v - hi
    mid = rest.astype(BF16).astype(F32)
    return [hi, mid, (rest - mid).astype(BF16).astype(F32)]


def kernel(
    n, nb, cap, lists, spots,
    plen_hbm, slen_hbm, owner_hbm, slot_hbm, q, kv, pool, x_hbm, b_hbm, c_hbm, dt_hbm, rate_hbm, skip_hbm, prior_hbm,
    attn_o, ssm_o,
    plen, slen, owner, slot, b_rows, c_rows, dt_t, rate, skip, code, codes, praw, pf_k, pf_v, pmat, sendbuf, recv, qbuf, kbuf, vbuf, kx, vt, vpart, mbuf, lbuf, accbuf, wbuf, obuf, ostage,
    x, prior, afull, skipf, xp, sbuf, hin, hout,
    loc, small, cs, cr, ps, pr, qs, qr, ks, kr, vs, vr, os, orr, hs, hr,
):
    me = lax.axis_index("cache")
    j = lax.axis_index("blk")
    tok = x.shape[0]
    wide = x.shape[1]
    width = GROUP * HD
    half = KVH * HD
    lanes = code.shape[1]
    rows = GROUP * tok
    part = 2 * HD
    parts = wide // part

    def unrolled(count, body):
        for i in range(count):
            body(i, 0)

    def zpeer(d):
        return lax.rem(me + d, n)

    def bpeer(e):
        return lax.rem(j + e, nb)

    def cols(at, size):
        return pl.ds(at if isinstance(at, int) else pl.multiple_of(at, 128), size)

    loads = [
        pltpu.make_async_copy(pool.at[:, cols(j * HD, HD)], praw.at[0], loc.at[0]),
        pltpu.make_async_copy(pool.at[:, cols(half + j * HD, HD)], praw.at[1], loc.at[1]),
        pltpu.make_async_copy(x_hbm, x, loc.at[2]),
        pltpu.make_async_copy(q.at[:, cols(j * width, width)], qbuf.at[j], loc.at[3]),
        pltpu.make_async_copy(kv.at[:, cols(j * HD, HD)], kbuf.at[j], loc.at[4]),
        pltpu.make_async_copy(kv.at[:, cols(half + j * HD, HD)], vbuf.at[j], loc.at[5]),
    ]
    prior_load = pltpu.make_async_copy(prior_hbm, prior, loc.at[6])
    barrier = pltpu.get_barrier_semaphore()

    pairs = [
        (owner_hbm, owner), (slot_hbm, slot), (plen_hbm, plen), (slen_hbm, slen), (dt_hbm, dt_t),
        (rate_hbm, rate), (skip_hbm, skip), (b_hbm, b_rows), (c_hbm, c_rows),
    ]
    fetches = [pltpu.make_async_copy(src, dst, small.at[i]) for i, (src, dst) in enumerate(pairs)]
    fetches[0].start()
    fetches[1].start()
    def greet(k, carry):
        peer = {"cache": zpeer(k // nb), "blk": bpeer(k % nb)}
        pl.semaphore_signal(barrier, inc=1, device_id=peer, device_id_type=pl.DeviceIdType.MESH)
        return carry

    if n * nb <= 16:
        for k in range(1, n * nb):
            greet(k, 0)
    else:
        lax.fori_loop(1, n * nb, greet, 0)
    mine = iota((1, lanes), 1) // lists == j
    fetches[0].wait()
    fetches[1].wait()
    named_slots = slot[...] * n + owner[...]
    code[...] = jnp.where(mine, jnp.concatenate([named_slots] * nb, axis=1), 0)
    codes[me, j] = code[...]

    pl.semaphore_wait(barrier, n * nb - 1)

    def code_copy(k):
        peer = {"cache": zpeer(k // nb), "blk": bpeer(k % nb)}
        return remote(code, codes.at[me, j], cs.at[k], cr.at[k], peer)

    def q_copy(e):
        to = bpeer(e)
        return remote(q.at[:, cols(to * width, width)], qbuf.at[j], qs.at[e], qr.at[e], {"blk": to})

    def k_copy(e):
        to = bpeer(e)
        return remote(kv.at[:, cols(to * HD, HD)], kbuf.at[j], ks.at[e], kr.at[e], {"blk": to})

    def v_copy(e):
        to = bpeer(e)
        return remote(kv.at[:, cols(half + to * HD, HD)], vbuf.at[j], vs.at[e], vr.at[e], {"blk": to})

    def page_copy(d, c):
        at = pl.ds(0, PAGE * HD) if c == 0 else pl.ds(PAGE * HD + (c - 1) * PAGE * PD, PAGE * PD)
        return remote(sendbuf.at[d, :, at], recv.at[d, :, at], ps.at[d, c], pr.at[d, c], {"cache": zpeer(d)})

    def state_copy():
        return remote(hout, hin, hs, hr, {"blk": bpeer(1)})

    def out_copy(e, s):
        to = bpeer(e)
        return remote(obuf.at[s, to], ostage.at[s, j], os.at[e, s], orr.at[e, s], {"blk": to})

    def each(what, low, high):
        if high - low <= 16:
            for i in range(low, high):
                what(i)
            return

        def body(i, carry):
            what(i)
            return carry

        lax.fori_loop(low, high, body, 0)

    def each_code(what):
        each(what, 1, n * nb)

    each_code(lambda k: code_copy(k).start())
    for load in loads + fetches[2:]:
        load.start()

    @pl.when(j == 0)
    def _():
        prior_load.start()

    loads[0].wait()
    loads[1].wait()
    pf_k[...] = praw[0].astype(F32)
    pf_v[...] = praw[1].astype(F32)
    if spots < pmat.shape[0]:
        pmat[...] = jnp.zeros_like(pmat)
    values = []
    for i in range(PAGE):
        at = pl.ds(i, spots, stride=PAGE)
        pmat[0:spots, i * HD : (i + 1) * HD] = pf_k[at, :].astype(BF16)
        values.append(pf_v[at, :])
    for s in range(PIECES):
        for t in range(PAGE // PIECES):
            tile = [values[t * PIECES + k][:, s * PD : (s + 1) * PD] for k in range(PIECES)]
            at = PAGE * HD + s * PAGE * PD + t * HD
            pmat[0:spots, at : at + HD] = jnp.concatenate(tile, axis=1).astype(BF16)

    @pl.when(j == 0)
    def _():
        prior_load.wait()

        def fill(i, carry):
            at = cols(i * HD, HD)
            hin[:, at] = prior[at, :].T.astype(BF16)
            return carry

        unrolled(wide // HD, fill)

    before = jnp.where(iota((lanes, lanes), 0) < iota((lanes, lanes), 1), 1.0, 0.0).astype(BF16)

    def comb(r):
        both = jnp.sum(codes[r], axis=0)
        return lax.rem(both, n), both // n

    def ranked(named):
        flags = jnp.broadcast_to(jnp.where(named, 1.0, 0.0), (16, lanes)).astype(BF16)
        return nn(flags, before)[0:1].astype(jnp.int32)

    def onehot(flag):
        return jnp.where(flag, 1.0, 0.0).astype(BF16)

    each_code(lambda k: code_copy(k).wait_recv())
    spread_spots = pmat.shape[0]

    def chosen_for(d):
        owners, slots = comb(zpeer(d))
        named = owners == me
        place = onehot((ranked(named) == iota((cap, lanes), 0)) & named)
        wants = onehot(slots == iota((spread_spots, lanes), 0))
        return nt(place, wants).astype(BF16)

    def answer(d, chosen, c):
        low = 0 if c == 0 else PAGE * HD + (c - 1) * PAGE * PD
        high = PAGE * HD + c * PAGE * PD
        for at in range(low, high, part):
            sendbuf[d, :, at : at + part] = nn(chosen, pmat[:, at : at + part]).astype(BF16)
        page_copy(d, c).start()

    if n <= 8:
        wanted = [chosen_for(d) for d in range(1, n)]
        for c in range(1 + PIECES):
            for d in range(1, n):
                answer(d, wanted[d - 1], c)
    else:
        def answer_all(d):
            chosen = chosen_for(d)
            for c in range(1 + PIECES):
                answer(d, chosen, c)

        each(answer_all, 1, n)
    each(lambda e: (k_copy(e).start(), v_copy(e).start(), q_copy(e).start()), 1, nb)

    for fetch in fetches[2:]:
        fetch.wait()
    prefix_limit = plen[...]
    suffix_limit = slen[...]
    dt = dt_t[...].T
    fall = jnp.concatenate(thirds(dt * (-rate[...])), axis=0).astype(BF16)
    tri = jnp.where(iota((tok, 3 * tok), 0) >= lax.rem(iota((tok, 3 * tok), 1), tok), 1.0, 0.0).astype(BF16)
    logs = nn(tri, fall)
    gains = jnp.concatenate([jnp.exp(logs), jnp.broadcast_to(skip[...], (16, SH))], axis=0)
    a3 = jnp.concatenate(thirds(gains), axis=1).astype(BF16)
    b3 = jnp.concatenate(thirds(jnp.exp(-logs) * dt), axis=1).astype(BF16)
    lower = iota((tok, tok), 0) >= iota((tok, tok), 1)
    gram = jnp.where(lower, nt(c_rows[...], b_rows[...]), 0.0).astype(BF16)
    readout = jnp.concatenate([gram, c_rows[...]], axis=1)
    b_t = b_rows[...].astype(F32).T.astype(BF16)

    loads[2].wait()

    def own_block(i, carry):
        at = cols(i * part, part)
        heads = lax.rem(iota((3 * SH, part), 0), SH)
        spread = jnp.where(heads == iota((3 * SH, part), 1) // HP + i * (part // HP), 1.0, 0.0).astype(BF16)
        grown = nn(a3, spread)
        afull[:, at] = grown[0:tok]
        skipf[:, at] = grown[tok : tok + 8]
        scaled = (nn(b3, spread) * x[:, at].astype(F32)).astype(BF16)
        xp[:, at] = scaled
        sbuf[:, at] = nn(b_t, scaled)
        return carry

    unrolled(parts, own_block)

    def onward(i, carry):
        at = cols(i * part, part)
        hout[:, at] = (afull[tok - 1 : tok, at] * (hin[:, at].astype(F32) + sbuf[:, at])).astype(BF16)
        return carry

    @pl.when(j == 0)
    def _():
        unrolled(parts, onward)
        state_copy().start()

    owners, slots = comb(me)
    back = me - owners
    away = jnp.where(back < 0, back + n, back)
    rank = jnp.zeros((1, lanes), jnp.int32)

    def add_rank(d, rank):
        named = away == d
        return rank + jnp.where(named, ranked(named), 0)

    if n <= 8:
        for d in range(1, n):
            rank = add_rank(d, rank)
    else:
        rank = lax.fori_loop(1, n, add_rank, rank)
    page = iota((lanes, 1), 0)
    first_row = (lax.rem(page, lists) * nb + page // lists) * PAGE
    same = jnp.where(iota((lanes, lanes), 0) == iota((lanes, lanes), 1), 1.0, 0.0).astype(BF16)
    own_wants = onehot((slots == iota((spread_spots, lanes), 0)) & (away == 0))
    places = [onehot((rank == iota((cap, lanes), 0)) & (away == d)) for d in range(1, n)]

    def read_block():
        alive = j * tok + iota((tok, part), 0) < suffix_limit

        def body(i, carry):
            at = cols(i * part, part)
            both = jnp.concatenate([xp[:, at], hin[:, at]], axis=0)
            total = afull[:, at] * nn(readout, both) + skipf[0:1, at] * x[:, at].astype(F32)
            ssm_o[:, at] = jnp.where(alive, total, 0.0).astype(BF16)
            return carry

        unrolled(parts, body)

    def chain():
        state_copy().wait_recv()

        @pl.when(j < nb - 1)
        def _():
            unrolled(parts, onward)
            state_copy().start()

    pl.when(j == 1)(chain)

    rate2 = math.log2(math.e) / math.sqrt(HD)
    first_lane = iota((1, HD), 1) == 0
    one_column = jnp.broadcast_to(jnp.where(first_lane, 1.0, 0.0), (tok, HD)).astype(BF16)

    def queries(b):
        pieces = [jnp.concatenate([qbuf[b, :, h * HD : (h + 1) * HD], one_column], axis=1) for h in range(GROUP)]
        return jnp.concatenate(pieces, axis=0)

    def bias(visible, size):
        column = jnp.where(visible, 0.0, NEG)
        return jnp.where(first_lane, jnp.broadcast_to(column, (size, HD)), 0.0).astype(BF16)

    for load in loads[3:]:
        load.wait()
    each(lambda e: (k_copy(e).wait_recv(), v_copy(e).wait_recv(), q_copy(e).wait_recv()), 1, nb)

    for b in range(nb):
        kx[b * tok : (b + 1) * tok, 0:HD] = kbuf[b]
        kx[b * tok : (b + 1) * tok, HD : 2 * HD] = bias(b * tok + iota((tok, 1), 0) < suffix_limit, tok)
        vt[:, b * tok : (b + 1) * tok] = vbuf[b].astype(F32).T.astype(BF16)
    causal = jnp.where(iota((tok, rows), 0) <= lax.rem(iota((tok, rows), 1), tok), 0.0, NEG)
    for b in range(nb):
        count = (b + 1) * tok
        qb = queries(b)
        scores = nt(kx[0:count, :], qb)
        near = scores[count - tok :] + causal
        scores = near if b == 0 else jnp.concatenate([scores[: count - tok], near], axis=0)
        top = jnp.max(scores, axis=0, keepdims=True) * rate2
        weights = jnp.exp2(scores * rate2 - top)
        mbuf[b] = top
        lbuf[b] = jnp.sum(weights, axis=0, keepdims=True)
        accbuf[b] = nn(vt[:, 0:count], weights.astype(BF16))

    table = jnp.concatenate([own_wants] + places, axis=0)
    pick = nt(same, table).astype(BF16)
    if nb == 4:
        over = 1 + 2 * lax.rem(j + 1, 2)
        order = [2, over, nb - over, nb]
    else:
        order = list(range(1, nb + 1))

    def gathered(at):
        got = recv[1:n, :, at : at + part].reshape((n - 1) * cap, part)
        return nn(pick, jnp.concatenate([pmat[:, at : at + part], got], axis=0))

    count = PAGE * lanes
    for i in range(PAGE):
        kx[i * lanes : (i + 1) * lanes, HD : 2 * HD] = bias(first_row + i < prefix_limit, lanes)
    each(lambda d: page_copy(d, 0).wait_recv(), 1, n)
    for at in range(0, PAGE * HD, part):
        out = gathered(at).astype(BF16)
        i = at // HD
        kx[i * lanes : (i + 1) * lanes, 0:HD] = out[:, 0:HD]
        kx[(i + 1) * lanes : (i + 2) * lanes, 0:HD] = out[:, HD : 2 * HD]
    for b in range(nb):
        scores = nt(kx[0:count, :], queries(b))
        old = mbuf[b]
        top = jnp.maximum(jnp.max(scores, axis=0, keepdims=True) * rate2, old)
        weights = jnp.exp2(scores * rate2 - top)
        factor = jnp.exp2(old - top)
        total = jnp.sum(weights, axis=0, keepdims=True) + lbuf[b] * factor
        alive = b * tok + lax.rem(iota((1, rows), 1), tok) < suffix_limit
        lbuf[b] = jnp.where(alive, 1.0 / total, 0.0)
        accbuf[b] = accbuf[b] * factor
        wbuf[b] = weights.astype(BF16)

    pl.when(j == 2)(chain)

    for s in range(PIECES):
        if s == PIECES - 1:
            pl.when(j > 2)(chain)
            read_block()
        each(lambda d: page_copy(d, 1 + s).wait_recv(), 1, n)
        for i in range(PAGE * PD // part):
            out = gathered(PAGE * HD + s * PAGE * PD + i * part)
            for t in range(2):
                turned = out[:, t * HD : (t + 1) * HD].T.astype(BF16)
                for k in range(PIECES):
                    row = (2 * i + t) * PIECES + k
                    vpart[:, row * lanes : (row + 1) * lanes] = turned[k * PD : (k + 1) * PD]
        for turn, e in enumerate(order):
            b = bpeer(e)
            final = (nn(vpart[...], wbuf[b]) + accbuf[b, s * PD : (s + 1) * PD]) * lbuf[b]
            heads = jnp.concatenate([final[:, h * tok : (h + 1) * tok] for h in range(GROUP)], axis=0)
            result = heads.T.astype(BF16)
            if turn < nb - 1:
                obuf[s, b] = result
                out_copy(e, s).start()
            else:
                ostage[s, j] = result

    each_code(lambda k: code_copy(k).wait_send())
    each(lambda e: (q_copy(e).wait_send(), k_copy(e).wait_send(), v_copy(e).wait_send()), 1, nb)
    for c in range(1 + PIECES):
        each(lambda d: page_copy(d, c).wait_send(), 1, n)

    @pl.when(j < nb - 1)
    def _():
        state_copy().wait_send()

    for s in range(PIECES):
        each(lambda e: out_copy(e, s).wait(), 1, nb)
    for b in range(nb):
        for h in range(GROUP):
            pieces = [ostage[s, b, :, h * PD : (h + 1) * PD] for s in range(PIECES)]
            attn_o[:, b * width + h * HD : b * width + (h + 1) * HD] = jnp.concatenate(pieces, axis=1)


def local(
    queries, kv_new, page_pool, page_owner, page_slot, prefix_len, suffix_len,
    ssm_in, b_in, c_in, step_size, decay_rate, skip_gain, prior_state,
):
    n = lax.axis_size("cache")
    nb = lax.axis_size("blk")
    tok = queries.shape[1]
    lists = page_owner.shape[2]
    lanes = nb * lists
    cap = max(16, max(2, 2 * lists // n) * nb)
    spots = page_pool.shape[1]
    spread_spots = max(spots, 128)
    vmem = pl.BlockSpec(memory_space=pltpu.VMEM)
    hbm = pl.BlockSpec(memory_space=pltpu.HBM)
    dma = pltpu.SemaphoreType.DMA
    wide = SH * HP
    rows = GROUP * tok
    most = max(nb * tok, PAGE * lanes)
    results = (
        jax.ShapeDtypeStruct((tok, QH * HD), BF16),
        jax.ShapeDtypeStruct((tok, wide), BF16),
    )
    attn, ssm = pl.pallas_call(
        functools.partial(kernel, n, nb, cap, lists, spots),
        out_shape=tuple(pltpu.VMEM(r.shape, r.dtype) for r in results),
        in_specs=[hbm] * 14,
        out_specs=(vmem, vmem),
        scratch_shapes=[
            pltpu.VMEM((1, 1), jnp.int32),
            pltpu.VMEM((1, 1), jnp.int32),
            pltpu.VMEM((1, lists), jnp.int32),
            pltpu.VMEM((1, lists), jnp.int32),
            pltpu.VMEM((tok, NS), BF16),
            pltpu.VMEM((tok, NS), BF16),
            pltpu.VMEM((SH, tok), F32),
            pltpu.VMEM((1, SH), F32),
            pltpu.VMEM((1, SH), F32),
            pltpu.VMEM((1, lanes), jnp.int32),
            pltpu.VMEM((n, nb, 1, lanes), jnp.int32),
            pltpu.VMEM((2, spots * PAGE, HD), BF16),
            pltpu.VMEM((spots * PAGE, HD), F32),
            pltpu.VMEM((spots * PAGE, HD), F32),
            pltpu.VMEM((spread_spots, 2 * PAGE * HD), BF16),
            pltpu.VMEM((n, cap, 2 * PAGE * HD), BF16),
            pltpu.VMEM((n, cap, 2 * PAGE * HD), BF16),
            pltpu.VMEM((nb, tok, GROUP * HD), BF16),
            pltpu.VMEM((nb, tok, HD), BF16),
            pltpu.VMEM((nb, tok, HD), BF16),
            pltpu.VMEM((most, 2 * HD), BF16),
            pltpu.VMEM((HD, nb * tok), BF16),
            pltpu.VMEM((PD, PAGE * lanes), BF16),
            pltpu.VMEM((nb, 1, rows), F32),
            pltpu.VMEM((nb, 1, rows), F32),
            pltpu.VMEM((nb, HD, rows), F32),
            pltpu.VMEM((nb, PAGE * lanes, rows), BF16),
            pltpu.VMEM((PIECES, nb, tok, GROUP * PD), BF16),
            pltpu.VMEM((PIECES, nb, tok, GROUP * PD), BF16),
            pltpu.VMEM((tok, wide), BF16),
            pltpu.VMEM((wide, NS), F32),
            pltpu.VMEM((tok, wide), F32),
            pltpu.VMEM((8, wide), F32),
            pltpu.VMEM((tok, wide), BF16),
            pltpu.VMEM((NS, wide), F32),
            pltpu.VMEM((NS, wide), BF16),
            pltpu.VMEM((NS, wide), BF16),
            dma((7,)), dma((9,)), dma((n * nb,)), dma((n * nb,)), dma((n, 1 + PIECES)), dma((n, 1 + PIECES)),
            dma((nb,)), dma((nb,)), dma((nb,)), dma((nb,)), dma((nb,)), dma((nb,)),
            dma((nb, PIECES)), dma((nb, PIECES)), dma, dma,
        ],
        compiler_params=pltpu.CompilerParams(
            collective_id=0, has_side_effects=True, vmem_limit_bytes=56 * 1024 * 1024
        ),
    )(
        prefix_len[None], suffix_len[None], page_owner[0, 0, :, 0][None], page_slot[0], queries[0], kv_new[0],
        page_pool.reshape(spots * PAGE, 2 * KVH * HD), ssm_in[0], b_in[0], c_in[0], step_size[0].T,
        decay_rate[None, :], skip_gain[None, :], prior_state.reshape(wide, NS),
    )
    return attn[None], ssm[None]


def solution(mesh):
    in_specs = (
        P(("groups", "cache"), "blk", None),
        P(("groups", "cache"), "blk", None),
        P(("groups", "cache"), None, None, None),
        P(("groups", "cache"), "blk", None, None),
        P(("groups", "cache"), "blk", None),
        P(("groups", "cache")),
        P(("groups", "cache")),
        P(("groups", "cache"), "blk", None),
        P(("groups", "cache"), "blk", None),
        P(("groups", "cache"), "blk", None),
        P(("groups", "cache"), "blk", None),
        P(),
        P(),
        P(("groups", "cache"), None, None, None),
    )
    out_specs = (P(("groups", "cache"), "blk", None), P(("groups", "cache"), "blk", None))
    return jax.shard_map(local, mesh=mesh, in_specs=in_specs, out_specs=out_specs, check_vma=False)
```

```python
import functools
import math

import jax
import jax.numpy as jnp
from jax import lax
from jax.experimental import pallas as pl
from jax.experimental.pallas import tpu as pltpu
from jax.sharding import PartitionSpec as P

QH = 16
KVH = 4
HD = 128
SH = 32
HP = 64
NS = 128
PAGE = 8
GROUP = QH // KVH
NEG = -1e30
PIECES = 2
PD = HD // PIECES
F32 = jnp.float32
BF16 = jnp.bfloat16


def remote(src, dst, send_sem, recv_sem, device):
    return pltpu.make_async_remote_copy(
        src_ref=src,
        dst_ref=dst,
        send_sem=send_sem,
        recv_sem=recv_sem,
        device_id=device,
        device_id_type=pl.DeviceIdType.MESH,
    )


def nt(a, b):
    return lax.dot_general(a, b, (((1,), (1,)), ((), ())), preferred_element_type=F32)


def nn(a, b):
    return jnp.dot(a, b, preferred_element_type=F32)


def iota(shape, axis):
    return lax.broadcasted_iota(jnp.int32, shape, axis)


def thirds(v):
    hi = v.astype(BF16).astype(F32)
    rest = v - hi
    mid = rest.astype(BF16).astype(F32)
    return [hi, mid, (rest - mid).astype(BF16).astype(F32)]


def kernel(
    n, nb, cap, lists, spots,
    plen_hbm, slen_hbm, owner_hbm, slot_hbm, q, kv, pool, x_hbm, b_hbm, c_hbm, dt_hbm, rate_hbm, skip_hbm, prior_hbm,
    both_o,
    plen, slen, owner, slot, b_rows, c_rows, dt_t, rate, skip, code, codes, praw, pf_k, pf_v, pmat, sendbuf, recv, qbuf, kbuf, vbuf, kx, vt, vpart, mbuf, lbuf, accbuf, wbuf, obuf, ostage,
    x, prior, afull, skipf, xp, sbuf, hin, hout,
    loc, small, cs, cr, ps, pr, qs, qr, ks, kr, vs, vr, os, orr, hs, hr,
):
    me = lax.axis_index("cache")
    j = lax.axis_index("blk")
    tok = x.shape[0]
    wide = x.shape[1]
    width = GROUP * HD
    half = KVH * HD
    lanes = code.shape[1]
    rows = GROUP * tok
    part = 2 * HD
    parts = wide // part

    def unrolled(count, body):
        for i in range(count):
            body(i, 0)

    def zpeer(d):
        return lax.rem(me + d, n)

    def bpeer(e):
        return lax.rem(j + e, nb)

    def cols(at, size):
        return pl.ds(at if isinstance(at, int) else pl.multiple_of(at, 128), size)

    loads = [
        pltpu.make_async_copy(pool.at[:, cols(j * HD, HD)], praw.at[0], loc.at[0]),
        pltpu.make_async_copy(pool.at[:, cols(half + j * HD, HD)], praw.at[1], loc.at[1]),
        pltpu.make_async_copy(x_hbm, x, loc.at[2]),
        pltpu.make_async_copy(q.at[:, cols(j * width, width)], qbuf.at[j], loc.at[3]),
        pltpu.make_async_copy(kv.at[:, cols(j * HD, HD)], kbuf.at[j], loc.at[4]),
        pltpu.make_async_copy(kv.at[:, cols(half + j * HD, HD)], vbuf.at[j], loc.at[5]),
    ]
    prior_load = pltpu.make_async_copy(prior_hbm, prior, loc.at[6])
    barrier = pltpu.get_barrier_semaphore()

    pairs = [
        (owner_hbm, owner), (slot_hbm, slot), (plen_hbm, plen), (slen_hbm, slen), (dt_hbm, dt_t),
        (rate_hbm, rate), (skip_hbm, skip), (b_hbm, b_rows), (c_hbm, c_rows),
    ]
    fetches = [pltpu.make_async_copy(src, dst, small.at[i]) for i, (src, dst) in enumerate(pairs)]
    fetches[0].start()
    fetches[1].start()
    def greet(k, carry):
        peer = {"cache": zpeer(k // nb), "blk": bpeer(k % nb)}
        pl.semaphore_signal(barrier, inc=1, device_id=peer, device_id_type=pl.DeviceIdType.MESH)
        return carry

    if n * nb <= 16:
        for k in range(1, n * nb):
            greet(k, 0)
    else:
        lax.fori_loop(1, n * nb, greet, 0)
    mine = iota((1, lanes), 1) // lists == j
    fetches[0].wait()
    fetches[1].wait()
    named_slots = slot[...] * n + owner[...]
    code[...] = jnp.where(mine, jnp.concatenate([named_slots] * nb, axis=1), 0)
    codes[me, j] = code[...]

    pl.semaphore_wait(barrier, n * nb - 1)

    def code_copy(k):
        peer = {"cache": zpeer(k // nb), "blk": bpeer(k % nb)}
        return remote(code, codes.at[me, j], cs.at[k], cr.at[k], peer)

    def q_copy(e):
        to = bpeer(e)
        return remote(q.at[:, cols(to * width, width)], qbuf.at[j], qs.at[e], qr.at[e], {"blk": to})

    def k_copy(e):
        to = bpeer(e)
        return remote(kv.at[:, cols(to * HD, HD)], kbuf.at[j], ks.at[e], kr.at[e], {"blk": to})

    def v_copy(e):
        to = bpeer(e)
        return remote(kv.at[:, cols(half + to * HD, HD)], vbuf.at[j], vs.at[e], vr.at[e], {"blk": to})

    def page_copy(d, c):
        at = pl.ds(0, PAGE * HD) if c == 0 else pl.ds(PAGE * HD + (c - 1) * PAGE * PD, PAGE * PD)
        return remote(sendbuf.at[d, :, at], recv.at[d, :, at], ps.at[d, c], pr.at[d, c], {"cache": zpeer(d)})

    def state_copy():
        return remote(hout, hin, hs, hr, {"blk": bpeer(1)})

    def out_copy(e, s):
        to = bpeer(e)
        return remote(obuf.at[s, to], ostage.at[s, j], os.at[e, s], orr.at[e, s], {"blk": to})

    def each(what, low, high):
        if high - low <= 16:
            for i in range(low, high):
                what(i)
            return

        def body(i, carry):
            what(i)
            return carry

        lax.fori_loop(low, high, body, 0)

    def each_code(what):
        each(what, 1, n * nb)

    each_code(lambda k: code_copy(k).start())
    for load in loads + fetches[2:]:
        load.start()

    @pl.when(j == 0)
    def _():
        prior_load.start()

    loads[0].wait()
    loads[1].wait()
    pf_k[...] = praw[0].astype(F32)
    pf_v[...] = praw[1].astype(F32)
    if spots < pmat.shape[0]:
        pmat[...] = jnp.zeros_like(pmat)
    for i in range(PAGE):
        at = pl.ds(i, spots, stride=PAGE)
        pmat[0:spots, i * HD : (i + 1) * HD] = pf_k[at, :].astype(BF16)
    @pl.when(j == 0)
    def _():
        prior_load.wait()

        def fill(i, carry):
            at = cols(i * HD, HD)
            hin[:, at] = prior[at, :].T.astype(BF16)
            return carry

        unrolled(wide // HD, fill)

    before = jnp.where(iota((lanes, lanes), 0) < iota((lanes, lanes), 1), 1.0, 0.0).astype(BF16)

    def comb(r):
        both = jnp.sum(codes[r], axis=0)
        return lax.rem(both, n), both // n

    def ranked(named):
        flags = jnp.broadcast_to(jnp.where(named, 1.0, 0.0), (16, lanes)).astype(BF16)
        return nn(flags, before)[0:1].astype(jnp.int32)

    def onehot(flag):
        return jnp.where(flag, 1.0, 0.0).astype(BF16)

    each_code(lambda k: code_copy(k).wait_recv())
    spread_spots = pmat.shape[0]

    def lay_values():
        values = [pf_v[pl.ds(i, spots, stride=PAGE), :] for i in range(PAGE)]
        for s in range(PIECES):
            for t in range(PAGE // PIECES):
                tile = [values[t * PIECES + k][:, s * PD : (s + 1) * PD] for k in range(PIECES)]
                at = PAGE * HD + s * PAGE * PD + t * HD
                pmat[0:spots, at : at + HD] = jnp.concatenate(tile, axis=1).astype(BF16)

    def chosen_for(d):
        owners, slots = comb(zpeer(d))
        named = owners == me
        place = onehot((ranked(named) == iota((cap, lanes), 0)) & named)
        wants = onehot(slots == iota((spread_spots, lanes), 0))
        return nt(place, wants).astype(BF16)

    def answer(d, chosen, c):
        low = 0 if c == 0 else PAGE * HD + (c - 1) * PAGE * PD
        high = PAGE * HD + c * PAGE * PD
        for at in range(low, high, part):
            sendbuf[d, :, at : at + part] = nn(chosen, pmat[:, at : at + part]).astype(BF16)
        page_copy(d, c).start()

    if n <= 8:
        far = 1 + 2 * lax.rem(me + 1, 2)
        turns = [2, far, n - far] if n == 4 else list(range(1, n))
        wanted = [chosen_for(d) for d in turns]
        for c in range(1 + PIECES):
            if c == 1:
                lay_values()
            for d, chosen in zip(turns, wanted):
                answer(d, chosen, c)
    else:
        lay_values()

        def answer_all(d):
            chosen = chosen_for(d)
            for c in range(1 + PIECES):
                answer(d, chosen, c)

        each(answer_all, 1, n)
    each(lambda e: (k_copy(e).start(), v_copy(e).start(), q_copy(e).start()), 1, nb)

    for fetch in fetches[2:]:
        fetch.wait()
    prefix_limit = plen[...]
    suffix_limit = slen[...]
    dt = dt_t[...].T
    fall = jnp.concatenate(thirds(dt * (-rate[...])), axis=0).astype(BF16)
    tri = jnp.where(iota((tok, 3 * tok), 0) >= lax.rem(iota((tok, 3 * tok), 1), tok), 1.0, 0.0).astype(BF16)
    logs = nn(tri, fall)
    gains = jnp.concatenate([jnp.exp(logs), jnp.broadcast_to(skip[...], (16, SH))], axis=0)
    a3 = jnp.concatenate(thirds(gains), axis=1).astype(BF16)
    b3 = jnp.concatenate(thirds(jnp.exp(-logs) * dt), axis=1).astype(BF16)
    lower = iota((tok, tok), 0) >= iota((tok, tok), 1)
    gram = jnp.where(lower, nt(c_rows[...], b_rows[...]), 0.0).astype(BF16)
    readout = jnp.concatenate([gram, c_rows[...]], axis=1)
    b_t = b_rows[...].astype(F32).T.astype(BF16)

    loads[2].wait()

    def own_block(i, carry):
        at = cols(i * part, part)
        heads = lax.rem(iota((3 * SH, part), 0), SH)
        spread = jnp.where(heads == iota((3 * SH, part), 1) // HP + i * (part // HP), 1.0, 0.0).astype(BF16)
        grown = nn(a3, spread)
        afull[:, at] = grown[0:tok]
        skipf[:, at] = grown[tok : tok + 8]
        scaled = (nn(b3, spread) * x[:, at].astype(F32)).astype(BF16)
        xp[:, at] = scaled
        sbuf[:, at] = nn(b_t, scaled)
        return carry

    unrolled(parts, own_block)

    def onward(i, carry):
        at = cols(i * part, part)
        hout[:, at] = (afull[tok - 1 : tok, at] * (hin[:, at].astype(F32) + sbuf[:, at])).astype(BF16)
        return carry

    @pl.when(j == 0)
    def _():
        unrolled(parts, onward)
        state_copy().start()

    owners, slots = comb(me)
    back = me - owners
    away = jnp.where(back < 0, back + n, back)
    rank = jnp.zeros((1, lanes), jnp.int32)

    def add_rank(d, rank):
        named = away == d
        return rank + jnp.where(named, ranked(named), 0)

    if n <= 8:
        for d in range(1, n):
            rank = add_rank(d, rank)
    else:
        rank = lax.fori_loop(1, n, add_rank, rank)
    page = iota((lanes, 1), 0)
    first_row = (lax.rem(page, lists) * nb + page // lists) * PAGE
    same = jnp.where(iota((lanes, lanes), 0) == iota((lanes, lanes), 1), 1.0, 0.0).astype(BF16)
    own_wants = onehot((slots == iota((spread_spots, lanes), 0)) & (away == 0))
    places = [onehot((rank == iota((cap, lanes), 0)) & (away == d)) for d in range(1, n)]

    def read_block():
        alive = j * tok + iota((tok, part), 0) < suffix_limit

        def body(i, carry):
            at = cols(i * part, part)
            both = jnp.concatenate([xp[:, at], hin[:, at]], axis=0)
            total = afull[:, at] * nn(readout, both) + skipf[0:1, at] * x[:, at].astype(F32)
            both_o[1, :, at] = jnp.where(alive, total, 0.0).astype(BF16)
            return carry

        unrolled(parts, body)

    def chain():
        state_copy().wait_recv()

        @pl.when(j < nb - 1)
        def _():
            unrolled(parts, onward)
            state_copy().start()

    pl.when(j == 1)(chain)

    rate2 = math.log2(math.e) / math.sqrt(HD)
    first_lane = iota((1, HD), 1) == 0
    one_column = jnp.broadcast_to(jnp.where(first_lane, 1.0, 0.0), (tok, HD)).astype(BF16)

    def queries(b):
        pieces = [jnp.concatenate([qbuf[b, :, h * HD : (h + 1) * HD], one_column], axis=1) for h in range(GROUP)]
        return jnp.concatenate(pieces, axis=0)

    def bias(visible, size):
        column = jnp.where(visible, 0.0, NEG)
        return jnp.where(first_lane, jnp.broadcast_to(column, (size, HD)), 0.0).astype(BF16)

    for load in loads[3:]:
        load.wait()
    each(lambda e: (k_copy(e).wait_recv(), v_copy(e).wait_recv(), q_copy(e).wait_recv()), 1, nb)

    for b in range(nb):
        kx[b * tok : (b + 1) * tok, 0:HD] = kbuf[b]
        kx[b * tok : (b + 1) * tok, HD : 2 * HD] = bias(b * tok + iota((tok, 1), 0) < suffix_limit, tok)
        vt[:, b * tok : (b + 1) * tok] = vbuf[b].astype(F32).T.astype(BF16)
    causal = jnp.where(iota((tok, rows), 0) <= lax.rem(iota((tok, rows), 1), tok), 0.0, NEG)
    for b in range(nb):
        count = (b + 1) * tok
        qb = queries(b)
        scores = nt(kx[0:count, :], qb)
        near = scores[count - tok :] + causal
        scores = near if b == 0 else jnp.concatenate([scores[: count - tok], near], axis=0)
        top = jnp.max(scores, axis=0, keepdims=True) * rate2
        weights = jnp.exp2(scores * rate2 - top)
        mbuf[b] = top
        lbuf[b] = jnp.sum(weights, axis=0, keepdims=True)
        accbuf[b] = nn(vt[:, 0:count], weights.astype(BF16))

    table = jnp.concatenate([own_wants] + places, axis=0)
    pick = nt(same, table).astype(BF16)
    if nb == 4:
        over = 1 + 2 * lax.rem(j + 1, 2)
        order = [2, over, nb - over, nb]
    else:
        order = list(range(1, nb + 1))

    def gathered(at):
        got = recv[1:n, :, at : at + part].reshape((n - 1) * cap, part)
        return nn(pick, jnp.concatenate([pmat[:, at : at + part], got], axis=0))

    count = PAGE * lanes
    for i in range(PAGE):
        kx[i * lanes : (i + 1) * lanes, HD : 2 * HD] = bias(first_row + i < prefix_limit, lanes)
    each(lambda d: page_copy(d, 0).wait_recv(), 1, n)
    for at in range(0, PAGE * HD, part):
        out = gathered(at).astype(BF16)
        i = at // HD
        kx[i * lanes : (i + 1) * lanes, 0:HD] = out[:, 0:HD]
        kx[(i + 1) * lanes : (i + 2) * lanes, 0:HD] = out[:, HD : 2 * HD]
    for b in range(nb):
        scores = nt(kx[0:count, :], queries(b))
        old = mbuf[b]
        top = jnp.maximum(jnp.max(scores, axis=0, keepdims=True) * rate2, old)
        weights = jnp.exp2(scores * rate2 - top)
        factor = jnp.exp2(old - top)
        total = jnp.sum(weights, axis=0, keepdims=True) + lbuf[b] * factor
        alive = b * tok + lax.rem(iota((1, rows), 1), tok) < suffix_limit
        lbuf[b] = jnp.where(alive, 1.0 / total, 0.0)
        accbuf[b] = accbuf[b] * factor
        wbuf[b] = weights.astype(BF16)

    pl.when(j == 2)(chain)

    for s in range(PIECES):
        if s == PIECES - 1:
            pl.when(j > 2)(chain)
            read_block()
        each(lambda d: page_copy(d, 1 + s).wait_recv(), 1, n)
        for i in range(PAGE * PD // part):
            out = gathered(PAGE * HD + s * PAGE * PD + i * part)
            for t in range(2):
                turned = out[:, t * HD : (t + 1) * HD].T.astype(BF16)
                for k in range(PIECES):
                    row = (2 * i + t) * PIECES + k
                    vpart[:, row * lanes : (row + 1) * lanes] = turned[k * PD : (k + 1) * PD]
        for turn, e in enumerate(order):
            b = bpeer(e)
            final = (nn(vpart[...], wbuf[b]) + accbuf[b, s * PD : (s + 1) * PD]) * lbuf[b]
            heads = jnp.concatenate([final[:, h * tok : (h + 1) * tok] for h in range(GROUP)], axis=0)
            result = heads.T.astype(BF16)
            if turn < nb - 1:
                obuf[s, b] = result
                out_copy(e, s).start()
            else:
                ostage[s, j] = result

    each_code(lambda k: code_copy(k).wait_send())
    each(lambda e: (q_copy(e).wait_send(), k_copy(e).wait_send(), v_copy(e).wait_send()), 1, nb)
    for c in range(1 + PIECES):
        each(lambda d: page_copy(d, c).wait_send(), 1, n)

    @pl.when(j < nb - 1)
    def _():
        state_copy().wait_send()

    for s in range(PIECES):
        each(lambda e: out_copy(e, s).wait(), 1, nb)
    for b in range(nb):
        for h in range(GROUP):
            pieces = [ostage[s, b, :, h * PD : (h + 1) * PD] for s in range(PIECES)]
            both_o[0, :, b * width + h * HD : b * width + (h + 1) * HD] = jnp.concatenate(pieces, axis=1)


def local(
    queries, kv_new, page_pool, page_owner, page_slot, prefix_len, suffix_len,
    ssm_in, b_in, c_in, step_size, decay_rate, skip_gain, prior_state,
):
    n = lax.axis_size("cache")
    nb = lax.axis_size("blk")
    tok = queries.shape[1]
    lists = page_owner.shape[2]
    lanes = nb * lists
    cap = max(16, max(2, 2 * lists // n) * nb)
    spots = page_pool.shape[1]
    spread_spots = max(spots, 128)
    vmem = pl.BlockSpec(memory_space=pltpu.VMEM)
    hbm = pl.BlockSpec(memory_space=pltpu.HBM)
    dma = pltpu.SemaphoreType.DMA
    wide = SH * HP
    rows = GROUP * tok
    most = max(nb * tok, PAGE * lanes)
    both = pl.pallas_call(
        functools.partial(kernel, n, nb, cap, lists, spots),
        out_shape=pltpu.VMEM((2, tok, wide), BF16),
        in_specs=[hbm] * 14,
        out_specs=vmem,
        scratch_shapes=[
            pltpu.VMEM((1, 1), jnp.int32),
            pltpu.VMEM((1, 1), jnp.int32),
            pltpu.VMEM((1, lists), jnp.int32),
            pltpu.VMEM((1, lists), jnp.int32),
            pltpu.VMEM((tok, NS), BF16),
            pltpu.VMEM((tok, NS), BF16),
            pltpu.VMEM((SH, tok), F32),
            pltpu.VMEM((1, SH), F32),
            pltpu.VMEM((1, SH), F32),
            pltpu.VMEM((1, lanes), jnp.int32),
            pltpu.VMEM((n, nb, 1, lanes), jnp.int32),
            pltpu.VMEM((2, spots * PAGE, HD), BF16),
            pltpu.VMEM((spots * PAGE, HD), F32),
            pltpu.VMEM((spots * PAGE, HD), F32),
            pltpu.VMEM((spread_spots, 2 * PAGE * HD), BF16),
            pltpu.VMEM((n, cap, 2 * PAGE * HD), BF16),
            pltpu.VMEM((n, cap, 2 * PAGE * HD), BF16),
            pltpu.VMEM((nb, tok, GROUP * HD), BF16),
            pltpu.VMEM((nb, tok, HD), BF16),
            pltpu.VMEM((nb, tok, HD), BF16),
            pltpu.VMEM((most, 2 * HD), BF16),
            pltpu.VMEM((HD, nb * tok), BF16),
            pltpu.VMEM((PD, PAGE * lanes), BF16),
            pltpu.VMEM((nb, 1, rows), F32),
            pltpu.VMEM((nb, 1, rows), F32),
            pltpu.VMEM((nb, HD, rows), F32),
            pltpu.VMEM((nb, PAGE * lanes, rows), BF16),
            pltpu.VMEM((PIECES, nb, tok, GROUP * PD), BF16),
            pltpu.VMEM((PIECES, nb, tok, GROUP * PD), BF16),
            pltpu.VMEM((tok, wide), BF16),
            pltpu.VMEM((wide, NS), F32),
            pltpu.VMEM((tok, wide), F32),
            pltpu.VMEM((8, wide), F32),
            pltpu.VMEM((tok, wide), BF16),
            pltpu.VMEM((NS, wide), F32),
            pltpu.VMEM((NS, wide), BF16),
            pltpu.VMEM((NS, wide), BF16),
            dma((7,)), dma((9,)), dma((n * nb,)), dma((n * nb,)), dma((n, 1 + PIECES)), dma((n, 1 + PIECES)),
            dma((nb,)), dma((nb,)), dma((nb,)), dma((nb,)), dma((nb,)), dma((nb,)),
            dma((nb, PIECES)), dma((nb, PIECES)), dma, dma,
        ],
        compiler_params=pltpu.CompilerParams(
            collective_id=0, has_side_effects=True, vmem_limit_bytes=56 * 1024 * 1024
        ),
    )(
        prefix_len[None], suffix_len[None], page_owner[0, 0, :, 0][None], page_slot[0], queries[0], kv_new[0],
        page_pool.reshape(spots * PAGE, 2 * KVH * HD), ssm_in[0], b_in[0], c_in[0], step_size[0].T,
        decay_rate[None, :], skip_gain[None, :], prior_state.reshape(wide, NS),
    )
    return both[0:1], both[1:2]


def solution(mesh):
    in_specs = (
        P(("groups", "cache"), "blk", None),
        P(("groups", "cache"), "blk", None),
        P(("groups", "cache"), None, None, None),
        P(("groups", "cache"), "blk", None, None),
        P(("groups", "cache"), "blk", None),
        P(("groups", "cache")),
        P(("groups", "cache")),
        P(("groups", "cache"), "blk", None),
        P(("groups", "cache"), "blk", None),
        P(("groups", "cache"), "blk", None),
        P(("groups", "cache"), "blk", None),
        P(),
        P(),
        P(("groups", "cache"), None, None, None),
    )
    out_specs = (P(("groups", "cache"), "blk", None), P(("groups", "cache"), "blk", None))
    return jax.shard_map(local, mesh=mesh, in_specs=in_specs, out_specs=out_specs, check_vma=False)
```

```python
import functools
import math

import jax
import jax.numpy as jnp
from jax import lax
from jax.experimental import pallas as pl
from jax.experimental.pallas import tpu as pltpu
from jax.sharding import PartitionSpec as P

QH = 16
KVH = 4
HD = 128
SH = 32
HP = 64
NS = 128
PAGE = 8
GROUP = QH // KVH
NEG = -1e30
PIECES = 2
PD = HD // PIECES
F32 = jnp.float32
BF16 = jnp.bfloat16


def remote(src, dst, send_sem, recv_sem, device):
    return pltpu.make_async_remote_copy(
        src_ref=src,
        dst_ref=dst,
        send_sem=send_sem,
        recv_sem=recv_sem,
        device_id=device,
        device_id_type=pl.DeviceIdType.MESH,
    )


def nt(a, b):
    return lax.dot_general(a, b, (((1,), (1,)), ((), ())), preferred_element_type=F32)


def nn(a, b):
    return jnp.dot(a, b, preferred_element_type=F32)


def iota(shape, axis):
    return lax.broadcasted_iota(jnp.int32, shape, axis)


def thirds(v):
    hi = v.astype(BF16).astype(F32)
    rest = v - hi
    mid = rest.astype(BF16).astype(F32)
    return [hi, mid, (rest - mid).astype(BF16).astype(F32)]


def kernel(
    n, nb, cap, lists, spots,
    plen_hbm, slen_hbm, owner_hbm, slot_hbm, q, kv, pool, x_hbm, b_hbm, c_hbm, dt_hbm, rate_hbm, skip_hbm, prior_hbm,
    both_o,
    plen, slen, owner, slot, b_rows, c_rows, dt_t, rate, skip, code, codes, praw, pf_k, pf_v, pmat, sendbuf, recv, qbuf, kbuf, vbuf, kx, vt, vpart, mbuf, lbuf, accbuf, wbuf, obuf, ostage,
    x, prior, afull, skipf, xp, sbuf, hin, hout,
    loc, small, cs, cr, ps, pr, qs, qr, ks, kr, vs, vr, os, orr, hs, hr,
):
    me = lax.axis_index("cache")
    j = lax.axis_index("blk")
    tok = x.shape[0]
    wide = x.shape[1]
    width = GROUP * HD
    half = KVH * HD
    lanes = code.shape[1]
    rows = GROUP * tok
    part = 2 * HD
    parts = wide // part

    def unrolled(count, body):
        for i in range(count):
            body(i, 0)

    def zpeer(d):
        return lax.rem(me + d, n)

    def bpeer(e):
        return lax.rem(j + e, nb)

    def cols(at, size):
        return pl.ds(at if isinstance(at, int) else pl.multiple_of(at, 128), size)

    loads = [
        pltpu.make_async_copy(pool.at[:, cols(j * HD, HD)], praw.at[0], loc.at[0]),
        pltpu.make_async_copy(pool.at[:, cols(half + j * HD, HD)], praw.at[1], loc.at[1]),
        pltpu.make_async_copy(x_hbm, x, loc.at[2]),
        pltpu.make_async_copy(q.at[:, cols(j * width, width)], qbuf.at[j], loc.at[3]),
        pltpu.make_async_copy(kv.at[:, cols(j * HD, HD)], kbuf.at[j], loc.at[4]),
        pltpu.make_async_copy(kv.at[:, cols(half + j * HD, HD)], vbuf.at[j], loc.at[5]),
    ]
    prior_load = pltpu.make_async_copy(prior_hbm, prior, loc.at[6])
    barrier = pltpu.get_barrier_semaphore()

    pairs = [
        (owner_hbm, owner), (slot_hbm, slot), (plen_hbm, plen), (slen_hbm, slen), (dt_hbm, dt_t),
        (rate_hbm, rate), (skip_hbm, skip), (b_hbm, b_rows), (c_hbm, c_rows),
    ]
    fetches = [pltpu.make_async_copy(src, dst, small.at[i]) for i, (src, dst) in enumerate(pairs)]
    fetches[0].start()
    fetches[1].start()
    def greet(k, carry):
        peer = {"cache": zpeer(k // nb), "blk": bpeer(k % nb)}
        pl.semaphore_signal(barrier, inc=1, device_id=peer, device_id_type=pl.DeviceIdType.MESH)
        return carry

    if n * nb <= 16:
        for k in list(range(nb, n * nb)) + list(range(1, nb)):
            greet(k, 0)
    else:
        lax.fori_loop(1, n * nb, greet, 0)
    mine = iota((1, lanes), 1) // lists == j
    fetches[0].wait()
    fetches[1].wait()
    named_slots = slot[...] * n + owner[...]
    code[...] = jnp.where(mine, jnp.concatenate([named_slots] * nb, axis=1), 0)
    codes[me, j] = code[...]

    pl.semaphore_wait(barrier, n * nb - 1)

    def code_copy(k):
        peer = {"cache": zpeer(k // nb), "blk": bpeer(k % nb)}
        return remote(code, codes.at[me, j], cs.at[k], cr.at[k], peer)

    def q_copy(e):
        to = bpeer(e)
        return remote(q.at[:, cols(to * width, width)], qbuf.at[j], qs.at[e], qr.at[e], {"blk": to})

    def k_copy(e):
        to = bpeer(e)
        return remote(kv.at[:, cols(to * HD, HD)], kbuf.at[j], ks.at[e], kr.at[e], {"blk": to})

    def v_copy(e):
        to = bpeer(e)
        return remote(kv.at[:, cols(half + to * HD, HD)], vbuf.at[j], vs.at[e], vr.at[e], {"blk": to})

    def page_copy(d, c):
        at = pl.ds(0, PAGE * HD) if c == 0 else pl.ds(PAGE * HD + (c - 1) * PAGE * PD, PAGE * PD)
        return remote(sendbuf.at[d, :, at], recv.at[d, :, at], ps.at[d, c], pr.at[d, c], {"cache": zpeer(d)})

    def state_copy():
        return remote(hout, hin, hs, hr, {"blk": bpeer(1)})

    def out_copy(e, s):
        to = bpeer(e)
        return remote(obuf.at[s, to], ostage.at[s, j], os.at[e, s], orr.at[e, s], {"blk": to})

    def each(what, low, high):
        if high - low <= 16:
            for i in range(low, high):
                what(i)
            return

        def body(i, carry):
            what(i)
            return carry

        lax.fori_loop(low, high, body, 0)

    def each_code(what):
        each(what, 1, n * nb)

    each(lambda k: code_copy(k).start(), nb, n * nb)
    each(lambda k: code_copy(k).start(), 1, nb)
    for load in loads + fetches[2:]:
        load.start()

    @pl.when(j == 0)
    def _():
        prior_load.start()

    loads[0].wait()
    loads[1].wait()
    pf_k[...] = praw[0].astype(F32)
    pf_v[...] = praw[1].astype(F32)
    if spots < pmat.shape[0]:
        pmat[...] = jnp.zeros_like(pmat)
    for i in range(PAGE):
        at = pl.ds(i, spots, stride=PAGE)
        pmat[0:spots, i * HD : (i + 1) * HD] = pf_k[at, :].astype(BF16)
    @pl.when(j == 0)
    def _():
        prior_load.wait()

        def fill(i, carry):
            at = cols(i * HD, HD)
            hin[:, at] = prior[at, :].T.astype(BF16)
            return carry

        unrolled(wide // HD, fill)

    before = jnp.where(iota((lanes, lanes), 0) < iota((lanes, lanes), 1), 1.0, 0.0).astype(BF16)

    def comb(r):
        both = jnp.sum(codes[r], axis=0)
        return lax.rem(both, n), both // n

    def ranked(named):
        flags = jnp.broadcast_to(jnp.where(named, 1.0, 0.0), (16, lanes)).astype(BF16)
        return nn(flags, before)[0:1].astype(jnp.int32)

    def onehot(flag):
        return jnp.where(flag, 1.0, 0.0).astype(BF16)

    each(lambda k: code_copy(k).wait_recv(), nb, n * nb)
    spread_spots = pmat.shape[0]

    def lay_values():
        values = [pf_v[pl.ds(i, spots, stride=PAGE), :] for i in range(PAGE)]
        for s in range(PIECES):
            for t in range(PAGE // PIECES):
                tile = [values[t * PIECES + k][:, s * PD : (s + 1) * PD] for k in range(PIECES)]
                at = PAGE * HD + s * PAGE * PD + t * HD
                pmat[0:spots, at : at + HD] = jnp.concatenate(tile, axis=1).astype(BF16)

    def chosen_for(d):
        owners, slots = comb(zpeer(d))
        named = owners == me
        place = onehot((ranked(named) == iota((cap, lanes), 0)) & named)
        wants = onehot(slots == iota((spread_spots, lanes), 0))
        return nt(place, wants).astype(BF16)

    def answer(d, chosen, c):
        low = 0 if c == 0 else PAGE * HD + (c - 1) * PAGE * PD
        high = PAGE * HD + c * PAGE * PD
        for at in range(low, high, part):
            sendbuf[d, :, at : at + part] = nn(chosen, pmat[:, at : at + part]).astype(BF16)
        page_copy(d, c).start()

    if n <= 8:
        far = 1 + 2 * lax.rem(me + 1, 2)
        turns = [2, far, n - far] if n == 4 else list(range(1, n))
        wanted = [chosen_for(d) for d in turns]
        for c in range(1 + PIECES):
            if c == 1:
                lay_values()
            for d, chosen in zip(turns, wanted):
                answer(d, chosen, c)
    else:
        lay_values()

        def answer_all(d):
            chosen = chosen_for(d)
            for c in range(1 + PIECES):
                answer(d, chosen, c)

        each(answer_all, 1, n)
    each(lambda e: (k_copy(e).start(), v_copy(e).start(), q_copy(e).start()), 1, nb)

    for fetch in fetches[2:]:
        fetch.wait()
    prefix_limit = plen[...]
    suffix_limit = slen[...]
    dt = dt_t[...].T
    fall = jnp.concatenate(thirds(dt * (-rate[...])), axis=0).astype(BF16)
    tri = jnp.where(iota((tok, 3 * tok), 0) >= lax.rem(iota((tok, 3 * tok), 1), tok), 1.0, 0.0).astype(BF16)
    logs = nn(tri, fall)
    gains = jnp.concatenate([jnp.exp(logs), jnp.broadcast_to(skip[...], (16, SH))], axis=0)
    a3 = jnp.concatenate(thirds(gains), axis=1).astype(BF16)
    b3 = jnp.concatenate(thirds(jnp.exp(-logs) * dt), axis=1).astype(BF16)
    lower = iota((tok, tok), 0) >= iota((tok, tok), 1)
    gram = jnp.where(lower, nt(c_rows[...], b_rows[...]), 0.0).astype(BF16)
    readout = jnp.concatenate([gram, c_rows[...]], axis=1)
    b_t = b_rows[...].astype(F32).T.astype(BF16)

    loads[2].wait()

    def own_block(i, carry):
        at = cols(i * part, part)
        heads = lax.rem(iota((3 * SH, part), 0), SH)
        spread = jnp.where(heads == iota((3 * SH, part), 1) // HP + i * (part // HP), 1.0, 0.0).astype(BF16)
        grown = nn(a3, spread)
        afull[:, at] = grown[0:tok]
        skipf[:, at] = grown[tok : tok + 8]
        scaled = (nn(b3, spread) * x[:, at].astype(F32)).astype(BF16)
        xp[:, at] = scaled
        sbuf[:, at] = nn(b_t, scaled)
        return carry

    unrolled(parts, own_block)

    def onward(i, carry):
        at = cols(i * part, part)
        hout[:, at] = (afull[tok - 1 : tok, at] * (hin[:, at].astype(F32) + sbuf[:, at])).astype(BF16)
        return carry

    @pl.when(j == 0)
    def _():
        unrolled(parts, onward)
        state_copy().start()

    each(lambda k: code_copy(k).wait_recv(), 1, nb)

    owners, slots = comb(me)
    back = me - owners
    away = jnp.where(back < 0, back + n, back)
    rank = jnp.zeros((1, lanes), jnp.int32)

    def add_rank(d, rank):
        named = away == d
        return rank + jnp.where(named, ranked(named), 0)

    if n <= 8:
        for d in range(1, n):
            rank = add_rank(d, rank)
    else:
        rank = lax.fori_loop(1, n, add_rank, rank)
    page = iota((lanes, 1), 0)
    first_row = (lax.rem(page, lists) * nb + page // lists) * PAGE
    same = jnp.where(iota((lanes, lanes), 0) == iota((lanes, lanes), 1), 1.0, 0.0).astype(BF16)
    own_wants = onehot((slots == iota((spread_spots, lanes), 0)) & (away == 0))
    places = [onehot((rank == iota((cap, lanes), 0)) & (away == d)) for d in range(1, n)]

    def read_block():
        alive = j * tok + iota((tok, part), 0) < suffix_limit

        def body(i, carry):
            at = cols(i * part, part)
            both = jnp.concatenate([xp[:, at], hin[:, at]], axis=0)
            total = afull[:, at] * nn(readout, both) + skipf[0:1, at] * x[:, at].astype(F32)
            both_o[1, :, at] = jnp.where(alive, total, 0.0).astype(BF16)
            return carry

        unrolled(parts, body)

    def chain():
        state_copy().wait_recv()

        @pl.when(j < nb - 1)
        def _():
            unrolled(parts, onward)
            state_copy().start()

    pl.when(j == 1)(chain)

    rate2 = math.log2(math.e) / math.sqrt(HD)
    first_lane = iota((1, HD), 1) == 0
    one_column = jnp.broadcast_to(jnp.where(first_lane, 1.0, 0.0), (tok, HD)).astype(BF16)

    def queries(b):
        pieces = [jnp.concatenate([qbuf[b, :, h * HD : (h + 1) * HD], one_column], axis=1) for h in range(GROUP)]
        return jnp.concatenate(pieces, axis=0)

    def bias(visible, size):
        column = jnp.where(visible, 0.0, NEG)
        return jnp.where(first_lane, jnp.broadcast_to(column, (size, HD)), 0.0).astype(BF16)

    for load in loads[3:]:
        load.wait()
    each(lambda e: (k_copy(e).wait_recv(), v_copy(e).wait_recv(), q_copy(e).wait_recv()), 1, nb)

    for b in range(nb):
        kx[b * tok : (b + 1) * tok, 0:HD] = kbuf[b]
        kx[b * tok : (b + 1) * tok, HD : 2 * HD] = bias(b * tok + iota((tok, 1), 0) < suffix_limit, tok)
        vt[:, b * tok : (b + 1) * tok] = vbuf[b].astype(F32).T.astype(BF16)
    causal = jnp.where(iota((tok, rows), 0) <= lax.rem(iota((tok, rows), 1), tok), 0.0, NEG)
    for b in range(nb):
        count = (b + 1) * tok
        qb = queries(b)
        scores = nt(kx[0:count, :], qb)
        near = scores[count - tok :] + causal
        scores = near if b == 0 else jnp.concatenate([scores[: count - tok], near], axis=0)
        top = jnp.max(scores, axis=0, keepdims=True) * rate2
        weights = jnp.exp2(scores * rate2 - top)
        mbuf[b] = top
        lbuf[b] = jnp.sum(weights, axis=0, keepdims=True)
        accbuf[b] = nn(vt[:, 0:count], weights.astype(BF16))

    table = jnp.concatenate([own_wants] + places, axis=0)
    pick = nt(same, table).astype(BF16)
    if nb == 4:
        over = 1 + 2 * lax.rem(j + 1, 2)
        order = [2, over, nb - over, nb]
    else:
        order = list(range(1, nb + 1))

    def gathered(at):
        got = recv[1:n, :, at : at + part].reshape((n - 1) * cap, part)
        return nn(pick, jnp.concatenate([pmat[:, at : at + part], got], axis=0))

    count = PAGE * lanes
    for i in range(PAGE):
        kx[i * lanes : (i + 1) * lanes, HD : 2 * HD] = bias(first_row + i < prefix_limit, lanes)
    each(lambda d: page_copy(d, 0).wait_recv(), 1, n)
    for at in range(0, PAGE * HD, part):
        out = gathered(at).astype(BF16)
        i = at // HD
        kx[i * lanes : (i + 1) * lanes, 0:HD] = out[:, 0:HD]
        kx[(i + 1) * lanes : (i + 2) * lanes, 0:HD] = out[:, HD : 2 * HD]
    for b in range(nb):
        scores = nt(kx[0:count, :], queries(b))
        old = mbuf[b]
        top = jnp.maximum(jnp.max(scores, axis=0, keepdims=True) * rate2, old)
        weights = jnp.exp2(scores * rate2 - top)
        factor = jnp.exp2(old - top)
        total = jnp.sum(weights, axis=0, keepdims=True) + lbuf[b] * factor
        alive = b * tok + lax.rem(iota((1, rows), 1), tok) < suffix_limit
        lbuf[b] = jnp.where(alive, 1.0 / total, 0.0)
        accbuf[b] = accbuf[b] * factor
        wbuf[b] = weights.astype(BF16)

    pl.when(j == 2)(chain)

    for s in range(PIECES):
        if s == PIECES - 1:
            pl.when(j > 2)(chain)
            read_block()
        each(lambda d: page_copy(d, 1 + s).wait_recv(), 1, n)
        for i in range(PAGE * PD // part):
            out = gathered(PAGE * HD + s * PAGE * PD + i * part)
            for t in range(2):
                turned = out[:, t * HD : (t + 1) * HD].T.astype(BF16)
                for k in range(PIECES):
                    row = (2 * i + t) * PIECES + k
                    vpart[:, row * lanes : (row + 1) * lanes] = turned[k * PD : (k + 1) * PD]
        for turn, e in enumerate(order):
            b = bpeer(e)
            final = (nn(vpart[...], wbuf[b]) + accbuf[b, s * PD : (s + 1) * PD]) * lbuf[b]
            heads = jnp.concatenate([final[:, h * tok : (h + 1) * tok] for h in range(GROUP)], axis=0)
            result = heads.T.astype(BF16)
            if turn < nb - 1:
                obuf[s, b] = result
                out_copy(e, s).start()
            else:
                ostage[s, j] = result

    each_code(lambda k: code_copy(k).wait_send())
    each(lambda e: (q_copy(e).wait_send(), k_copy(e).wait_send(), v_copy(e).wait_send()), 1, nb)
    for c in range(1 + PIECES):
        each(lambda d: page_copy(d, c).wait_send(), 1, n)

    @pl.when(j < nb - 1)
    def _():
        state_copy().wait_send()

    for s in range(PIECES):
        each(lambda e: out_copy(e, s).wait(), 1, nb)
    for b in range(nb):
        for h in range(GROUP):
            pieces = [ostage[s, b, :, h * PD : (h + 1) * PD] for s in range(PIECES)]
            both_o[0, :, b * width + h * HD : b * width + (h + 1) * HD] = jnp.concatenate(pieces, axis=1)


def local(
    queries, kv_new, page_pool, page_owner, page_slot, prefix_len, suffix_len,
    ssm_in, b_in, c_in, step_size, decay_rate, skip_gain, prior_state,
):
    n = lax.axis_size("cache")
    nb = lax.axis_size("blk")
    tok = queries.shape[1]
    lists = page_owner.shape[2]
    lanes = nb * lists
    cap = max(16, max(2, 2 * lists // n) * nb)
    spots = page_pool.shape[1]
    spread_spots = max(spots, 128)
    vmem = pl.BlockSpec(memory_space=pltpu.VMEM)
    hbm = pl.BlockSpec(memory_space=pltpu.HBM)
    dma = pltpu.SemaphoreType.DMA
    wide = SH * HP
    rows = GROUP * tok
    most = max(nb * tok, PAGE * lanes)
    both = pl.pallas_call(
        functools.partial(kernel, n, nb, cap, lists, spots),
        out_shape=pltpu.VMEM((2, tok, wide), BF16),
        in_specs=[hbm] * 14,
        out_specs=vmem,
        scratch_shapes=[
            pltpu.VMEM((1, 1), jnp.int32),
            pltpu.VMEM((1, 1), jnp.int32),
            pltpu.VMEM((1, lists), jnp.int32),
            pltpu.VMEM((1, lists), jnp.int32),
            pltpu.VMEM((tok, NS), BF16),
            pltpu.VMEM((tok, NS), BF16),
            pltpu.VMEM((SH, tok), F32),
            pltpu.VMEM((1, SH), F32),
            pltpu.VMEM((1, SH), F32),
            pltpu.VMEM((1, lanes), jnp.int32),
            pltpu.VMEM((n, nb, 1, lanes), jnp.int32),
            pltpu.VMEM((2, spots * PAGE, HD), BF16),
            pltpu.VMEM((spots * PAGE, HD), F32),
            pltpu.VMEM((spots * PAGE, HD), F32),
            pltpu.VMEM((spread_spots, 2 * PAGE * HD), BF16),
            pltpu.VMEM((n, cap, 2 * PAGE * HD), BF16),
            pltpu.VMEM((n, cap, 2 * PAGE * HD), BF16),
            pltpu.VMEM((nb, tok, GROUP * HD), BF16),
            pltpu.VMEM((nb, tok, HD), BF16),
            pltpu.VMEM((nb, tok, HD), BF16),
            pltpu.VMEM((most, 2 * HD), BF16),
            pltpu.VMEM((HD, nb * tok), BF16),
            pltpu.VMEM((PD, PAGE * lanes), BF16),
            pltpu.VMEM((nb, 1, rows), F32),
            pltpu.VMEM((nb, 1, rows), F32),
            pltpu.VMEM((nb, HD, rows), F32),
            pltpu.VMEM((nb, PAGE * lanes, rows), BF16),
            pltpu.VMEM((PIECES, nb, tok, GROUP * PD), BF16),
            pltpu.VMEM((PIECES, nb, tok, GROUP * PD), BF16),
            pltpu.VMEM((tok, wide), BF16),
            pltpu.VMEM((wide, NS), F32),
            pltpu.VMEM((tok, wide), F32),
            pltpu.VMEM((8, wide), F32),
            pltpu.VMEM((tok, wide), BF16),
            pltpu.VMEM((NS, wide), F32),
            pltpu.VMEM((NS, wide), BF16),
            pltpu.VMEM((NS, wide), BF16),
            dma((7,)), dma((9,)), dma((n * nb,)), dma((n * nb,)), dma((n, 1 + PIECES)), dma((n, 1 + PIECES)),
            dma((nb,)), dma((nb,)), dma((nb,)), dma((nb,)), dma((nb,)), dma((nb,)),
            dma((nb, PIECES)), dma((nb, PIECES)), dma, dma,
        ],
        compiler_params=pltpu.CompilerParams(
            collective_id=0, has_side_effects=True, vmem_limit_bytes=56 * 1024 * 1024
        ),
    )(
        prefix_len[None], suffix_len[None], page_owner[0, 0, :, 0][None], page_slot[0], queries[0], kv_new[0],
        page_pool.reshape(spots * PAGE, 2 * KVH * HD), ssm_in[0], b_in[0], c_in[0], step_size[0].T,
        decay_rate[None, :], skip_gain[None, :], prior_state.reshape(wide, NS),
    )
    return both[0:1], both[1:2]


def solution(mesh):
    in_specs = (
        P(("groups", "cache"), "blk", None),
        P(("groups", "cache"), "blk", None),
        P(("groups", "cache"), None, None, None),
        P(("groups", "cache"), "blk", None, None),
        P(("groups", "cache"), "blk", None),
        P(("groups", "cache")),
        P(("groups", "cache")),
        P(("groups", "cache"), "blk", None),
        P(("groups", "cache"), "blk", None),
        P(("groups", "cache"), "blk", None),
        P(("groups", "cache"), "blk", None),
        P(),
        P(),
        P(("groups", "cache"), None, None, None),
    )
    out_specs = (P(("groups", "cache"), "blk", None), P(("groups", "cache"), "blk", None))
    return jax.shard_map(local, mesh=mesh, in_specs=in_specs, out_specs=out_specs, check_vma=False)
```
